32 devices in a mesh: row: 4 (over z), col: 8 (over y, x, core).
Axes of the slice: x: 2, y: 2, z: 4, core: 2. Of those that a mesh axis runs over, the one named last changes fastest.
Arguments:
- user_factors: bfloat16 [8192, 128], P(('row', 'col')), may hold values from -1.796875 to 1.796875
- item_factors: bfloat16 [8, 768, 128], P('col', 'row'), may hold values from -1.796875 to 1.796875
- ratings: bfloat16 [4, 8, 36, 128, 128], P('row', 'col'), may hold values from 0 to 8, as said below
- tile_cell: int32 [4, 8, 36], P('row', 'col'), may hold values from 0 to 95, as said below
- keep_count: int32 [4, 8], P('row', 'col'), may hold values from 1 to 32, as said below
- send_count: int32 [4, 8, 4], P('row', 'col'), may hold values from 0 to 2, as said below
- user_nbrs: int32 [8192, 16], P(('row', 'col')), may hold values from 0 to 2047
- item_nbrs: int32 [8, 768, 16], P('col', 'row'), may hold values from 0 to 767
Outputs:
- grad_users: float32 [8192, 128], P(('row', 'col'))
- grad_items: float32 [8, 768, 128], P('col', 'row')
The draws below stay inside these ranges and needn't reach their ends.
Inputs may be any that keep to these rules, and one draw needn't show every extreme that they name: `ratings`: zero marks an unobserved entry; a nonzero value is at least 0.25. `tile_cell`: cells are distinct within a device; cell a * 6 + b is user subtile a of the device's user block and item subtile b of its item block. keep_count plus the sum of send_count is at most 36 on every device and equals 36 on some device of every item block. `send_count`: A device assigns no slots to itself and at most 2 to each other device of its item block; the assigned slots follow its kept slots in the order of the receiving devices; some device assigns exactly 2 to some peer. `user_nbrs`: neighbours index rows of the user's own block. `item_nbrs`: neighbours index rows of the item's own block.
All inputs are finite; a program needn't handle non-finite values.
Results may differ from the reference program's by a relative error of at most 0.0012.
Values may be sent and summed in bfloat16 or wider, within the bound.
No kernel may reach another device: no remote copies, remote signals or barrier semaphores. Data moves between devices by JAX's collectives and lax.ppermute only.
A program may use at most 64 MiB of HBM per device.

```python
import jax
import jax.numpy as jnp
from jax import lax

RANK = 128
TILE = 128
UT = 16
VT = 6
SLOTS = 36
PEER = 2
KNN = 16
UBLK = 2048
USERS = 8192
VBLK = 768
N_ROW = 4
N_COL = 8


def tile_plan(key):
    base_key = jax.random.fold_in(key, 7301)
    heavy = jax.random.randint(jax.random.fold_in(base_key, 1), (N_COL,), 0, N_ROW)
    marked = jax.random.randint(jax.random.fold_in(base_key, 5), (), 0, N_COL)
    light = jax.random.randint(jax.random.fold_in(base_key, 2), (N_ROW, N_COL), SLOTS // 6, SLOTS // 3 + 1)
    rows = jnp.arange(N_ROW)[:, None]
    columns = jnp.arange(N_COL)[None, :]
    is_marked_col = columns == marked
    next_row = (heavy[None, :] + 1) % N_ROW
    light = jnp.where(is_marked_col & (rows == next_row), SLOTS // 3, light)
    is_heavy = rows == heavy[None, :]
    counts = jnp.where(is_heavy, SLOTS, light)
    peer_draw = jax.random.randint(jax.random.fold_in(base_key, 3), (N_ROW, N_COL, N_ROW), 1, PEER + 1)
    peer_draw = jnp.where(is_marked_col[:, :, None], 1, peer_draw)
    peers = jnp.arange(N_ROW)[None, None, :]
    owner = jnp.arange(N_ROW)[:, None, None]
    first = (owner + 1) % N_ROW
    per_peer = jnp.where(peers == first, PEER, peer_draw)
    per_peer = jnp.where(peers == owner, 0, per_peer)
    sends = jnp.where(is_heavy[:, :, None], per_peer, 0)
    keep = counts - jnp.sum(sends, axis=2)
    scores = jax.random.randint(jax.random.fold_in(base_key, 4), (N_ROW, N_COL, UT * VT), 0, 2 ** 20)
    scores = scores * (UT * VT) + jnp.arange(UT * VT)[None, None, :]
    order = jnp.argsort(scores, axis=2)
    cells = order[:, :, :SLOTS]
    return (cells.astype(jnp.int32), keep.astype(jnp.int32), sends.astype(jnp.int32))


def draw_tile_cell(key, part):
    return tile_plan(key)[0]


def draw_keep_count(key, part):
    return tile_plan(key)[1]


def draw_send_count(key, part):
    return tile_plan(key)[2]


def draw_ratings(key, part):
    shape = (N_ROW, N_COL, SLOTS, TILE, TILE)
    seen = jax.random.uniform(jax.random.fold_in(key, 11), shape) < 0.4
    level = jnp.exp(jax.random.uniform(jax.random.fold_in(key, 12), shape, minval=jnp.log(0.25), maxval=jnp.log(8.0)))
    return jnp.where(seen, level, 0.0).astype(jnp.float32).astype(jnp.bfloat16)


def place_ends(values, own_key, low, largest):
    index_at = [jax.random.randint(jax.random.fold_in(own_key, axis), (), 0, length) for axis, length in enumerate(values.shape)]
    longest = values.shape.index(max(values.shape))
    neighbour = index_at[:longest] + [(index_at[longest] + 1) % values.shape[longest]] + index_at[longest + 1:]
    return values.at[tuple(index_at)].set(low).at[tuple(neighbour)].set(largest)


def shard_levels(rng, shape, pieces, smallest, top_value):
    loudness, own = 1.0, jax.random.fold_in(rng, 6)
    for position, shards_of in pieces:
        heights = jnp.exp(jax.random.uniform(jax.random.fold_in(own, position), (shards_of,), jnp.float32, smallest / len(pieces), top_value / len(pieces)))
        loudness = loudness * jnp.repeat(heights, shape[position] // shards_of).reshape([-1 if axis == position else 1 for axis in range(len(shape))])
    return loudness


def bell_draw(key, dims, deviation, limit, cuts=(), held_as=jnp.bfloat16):
    factor_of = shard_levels(key, dims, cuts, -0.22, 0.18) if cuts else 1.0
    array = jax.random.normal(key, dims, jnp.float32) * deviation * factor_of
    return jnp.minimum(jnp.maximum(array, -limit), limit).astype(held_as)


def setup_inputs(seed: int = 0) -> dict:
    seeds = jax.random.split(jax.random.key(seed), 9)
    return {
        "user_factors": bell_draw(seeds[0], (USERS, RANK), 0.3, 1.796875, ((0, 32),)),
        "item_factors": bell_draw(seeds[1], (N_COL, VBLK, RANK), 0.3, 1.796875, ((0, 8), (1, 4))),
        "ratings": draw_ratings(jax.random.fold_in(seeds[8], 71), 0),
        "tile_cell": draw_tile_cell(jax.random.fold_in(seeds[8], 71), 0),
        "keep_count": draw_keep_count(jax.random.fold_in(seeds[8], 71), 0),
        "send_count": draw_send_count(jax.random.fold_in(seeds[8], 71), 0),
        "user_nbrs": place_ends(jax.random.randint(seeds[6], (USERS, KNN), 0, UBLK), jax.random.fold_in(seeds[6], 1), 0, UBLK - 1).astype(jnp.int32),
        "item_nbrs": place_ends(jax.random.randint(seeds[7], (N_COL, VBLK, KNN), 0, VBLK), jax.random.fold_in(seeds[7], 1), 0, VBLK - 1).astype(jnp.int32),
    }


ALPHA = 0.5
DATA_SCALE = 0.0625
SMOOTH = 4.0


def smoothing(blocks, neighbours):
    rows = blocks.astype(jnp.float32)
    near = jax.vmap(lambda block, index: jnp.take(block, index, axis=0))(rows, neighbours)
    return rows - jnp.sum(near, axis=2) / KNN


def reference(user_factors, item_factors, ratings, tile_cell, keep_count, send_count, user_nbrs, item_nbrs):
    user_tiles = user_factors.reshape(N_ROW, UT, TILE, RANK)
    counts = (keep_count + jnp.sum(send_count, axis=2)).astype(jnp.int32)

    def over_rows(item_acc, row_index):
        user_block = user_tiles[row_index]

        def over_cols(carry, col_index):
            user_acc, item_all = carry
            item_block = item_factors[col_index].reshape(VT, TILE, RANK)
            slot_ratings = ratings[row_index, col_index]
            slot_cells = tile_cell[row_index, col_index]

            def one_tile(slot, inner):
                user_part, item_part = inner
                cell = slot_cells[slot]
                upper = cell // VT
                lower = cell % VT
                left = user_block[upper]
                right = item_block[lower]
                product = jnp.dot(left, right.T, preferred_element_type=jnp.float32)
                values = slot_ratings[slot].astype(jnp.float32)
                prefer = jnp.where(values > 0, 1.0, 0.0).astype(jnp.float32)
                error = ((1.0 + ALPHA * values) * (product - prefer)).astype(jnp.bfloat16)
                user_part = user_part.at[upper].add(jnp.dot(error, right, preferred_element_type=jnp.float32))
                item_part = item_part.at[lower].add(jnp.dot(error.T, left, preferred_element_type=jnp.float32))
                return user_part, item_part

            item_col = item_all[col_index]
            user_acc, item_col = lax.fori_loop(0, counts[row_index, col_index], one_tile, (user_acc, item_col))
            item_all = item_all.at[col_index].set(item_col)
            return (user_acc, item_all), None

        start = (jnp.zeros((UT, TILE, RANK), jnp.float32), item_acc)
        (user_acc, item_acc), _ = lax.scan(over_cols, start, jnp.arange(N_COL))
        return item_acc, user_acc

    item_zero = jnp.zeros((N_COL, VT, TILE, RANK), jnp.float32)
    item_data, user_data = lax.scan(over_rows, item_zero, jnp.arange(N_ROW))
    user_smooth = smoothing(user_factors.reshape(N_ROW, UBLK, RANK), user_nbrs.reshape(N_ROW, UBLK, KNN))
    item_smooth = smoothing(item_factors, item_nbrs)
    grad_users = DATA_SCALE * user_data.reshape(USERS, RANK) + SMOOTH * user_smooth.reshape(USERS, RANK)
    grad_items = DATA_SCALE * item_data.reshape(N_COL, VBLK, RANK) + SMOOTH * item_smooth
    return grad_users, grad_items
```

```python
import functools

import jax
import jax.numpy as jnp
from jax import lax
from jax.experimental import pallas as pl
from jax.experimental.pallas import tpu as pltpu
from jax.sharding import PartitionSpec as P

ALPHA = 0.5
DATA_SCALE = 0.0625
SMOOTH = 4.0
GROUP = 4
VMEM = pl.BlockSpec(memory_space=pltpu.VMEM)
SMEM = pl.BlockSpec(memory_space=pltpu.SMEM)


def call(kernel, outs, ins, name, scratch=(), flops=0, nbytes=0, smem=0, limit=16):
    return pl.pallas_call(
        kernel,
        out_shape=outs,
        in_specs=[SMEM] * smem + [VMEM] * (len(ins) - smem),
        out_specs=jax.tree.map(lambda _: VMEM, outs),
        scratch_shapes=scratch,
        cost_estimate=pl.CostEstimate(flops=flops, bytes_accessed=nbytes, transcendentals=0),
        compiler_params=pltpu.CompilerParams(vmem_limit_bytes=limit * 2**20),
        name=name,
    )(*ins)


def struct(rows, cols, dtype):
    return jax.ShapeDtypeStruct((rows, cols), dtype)


EXTRA = 16
OCTAVE = 64.0
TOP = 32400.0


def encode(block, out_ref, start):
    rows = block.shape[0]
    top = jnp.max(jnp.abs(block), axis=0, keepdims=True)
    level = jnp.ceil(jnp.log2(jnp.maximum(top, 1e-30)) * OCTAVE)
    fixed = jnp.round(block * (jnp.exp2(level * (-1.0 / OCTAVE)) * TOP))
    out_ref[start : start + rows, :] = fixed.astype(jnp.int32).astype(jnp.int16)
    spread = jnp.broadcast_to(level, (EXTRA, block.shape[1]))
    out_ref[start + rows : start + rows + EXTRA, :] = spread.astype(jnp.int32).astype(jnp.int16)


def decode(ref):
    rows = ref.shape[0] - EXTRA
    level = ref[rows : rows + EXTRA, :].astype(jnp.int32).astype(jnp.float32)[:1]
    scale = jnp.exp2(level * (1.0 / OCTAVE)) * (1.0 / TOP)
    return ref[:rows, :].astype(jnp.int32).astype(jnp.float32) * scale


def adjacency_kernel(user_nbrs, item_nbrs, user_adj, item_adj):
    for nbrs, adj in ((user_nbrs, user_adj), (item_nbrs, item_adj)):
        rows, count = nbrs.shape
        step = 16

        def body(turn, _, nbrs=nbrs, adj=adj, step=step, count=count):
            at = pl.ds(pl.multiple_of(turn * step, step), step)
            index = nbrs[at, :]
            columns = [jnp.broadcast_to(index[:, k : k + 1], (step, 128)) for k in range(count)]
            lane = lax.broadcasted_iota(jnp.int32, (step, 128), 1)
            for block in range(adj.shape[1] // 128):
                here = lane + block * 128
                total = jnp.zeros((step, 128), jnp.float32)
                for column in columns:
                    total = total + jnp.where(column == here, 1.0, 0.0)
                adj[at, block * 128 : (block + 1) * 128] = total.astype(jnp.bfloat16)
            return 0

        lax.fori_loop(0, rows // step, body, 0)


def main_kernel(
    n_user, n_item, split, keep, sends, cells, ratings, *refs
):
    user_in, refs = refs[:n_user], refs[n_user:]
    item_in, refs = refs[:n_item], refs[n_item:]
    outs, (users, items, user_acc, item_acc) = refs[:-4], refs[-4:]
    tile = ratings.shape[1]
    item_count = items.shape[0] // tile
    place(user_in, users, "col")
    place(item_in, items, "row")
    user_acc[...] = jnp.zeros_like(user_acc)
    item_acc[...] = jnp.zeros_like(item_acc)
    live = keep[0, 0]
    for q in range(sends.shape[2]):
        live = live + sends[0, 0, q]

    def body(turn, _):
        work = []
        for g in range(GROUP):
            slot = turn * GROUP + g
            cell = cells[0, 0, slot]
            upper = cell // item_count
            lower = cell - upper * item_count
            user_at = pl.ds(pl.multiple_of(upper * tile, tile), tile)
            item_at = pl.ds(pl.multiple_of(lower * tile, tile), tile)
            left = users[user_at, :]
            right = items[item_at, :]
            product = lax.dot_general(
                left, right, (((1,), (1,)), ((), ())), preferred_element_type=jnp.float32
            )
            value = ratings[slot].astype(jnp.float32)
            error = (1.0 + ALPHA * value) * (product - jnp.where(value > 0, 1.0, 0.0))
            error = jnp.where(slot < live, error, 0.0).astype(jnp.bfloat16)
            work.append((user_at, item_at, left, right, error))
        for user_at, item_at, left, right, error in work:
            user_acc[user_at, :] += jnp.dot(error, right, preferred_element_type=jnp.float32)
            item_acc[item_at, :] += lax.dot_general(
                error, left, (((0,), (0,)), ((), ())), preferred_element_type=jnp.float32
            )
        return 0

    lax.fori_loop(0, (live + GROUP - 1) // GROUP, body, 0)

    if not split:
        outs[0][...] = user_acc[...]
        outs[1][...] = item_acc[...]
        return
    user_keep, user_send, item_keep, *item_send = outs
    me = lax.axis_index("col")
    rows = user_in[0].shape[0]
    for k in range(0, n_user, 2):
        for out, mask in ((user_keep, k), (user_send, k + 1)):
            at = pl.ds(pl.multiple_of((me ^ mask) * rows, rows), rows)
            out[k // 2 * rows : (k // 2 + 1) * rows, :] = user_acc[at, :]
    me = lax.axis_index("row")
    rows = item_in[0].shape[0]
    for k in range(n_item):
        at = pl.ds(pl.multiple_of((me ^ k) * rows, rows), rows)
        if k == 0:
            item_keep[...] = item_acc[at, :]
        else:
            encode(item_acc[at, :], item_send[k - 1], 0)


def place(shards, whole, axis):
    if len(shards) == 1:
        whole[...] = shards[0][...].reshape(whole.shape)
        return
    me = lax.axis_index(axis)
    rows = shards[0].shape[0]
    for k, shard in enumerate(shards):
        whole[pl.ds(pl.multiple_of((me ^ k) * rows, rows), rows), :] = shard[...]


def chip_sum_kernel(keep, recv, own, *sends):
    rows = own.shape[0]
    own[...] = keep[:rows, :] + recv[:rows, :]
    for k, send in enumerate(sends, 1):
        at = slice(k * rows, (k + 1) * rows)
        encode(keep[at, :] + recv[at, :], send, 0)


def smooth_kernel(n_user, n_item, user_adj, item_adj, user_own, item_own, *refs):
    user_in, refs = refs[:n_user], refs[n_user:]
    item_in, refs = refs[:n_item], refs[n_item:]
    user_out, item_out, users, items = refs
    place(user_in, users, "col")
    place(item_in, items, "row")
    for adj, whole, own, out in (
        (user_adj, users, user_own, user_out),
        (item_adj, items, item_own, item_out),
    ):
        near = jnp.dot(adj[...], whole[...], preferred_element_type=jnp.float32)
        out[...] = SMOOTH * (own[...].astype(jnp.float32) - near * (1.0 / 16))


def final_kernel(n_user, user_smooth, item_smooth, user_own, item_own, *refs):
    user_parts, item_parts, (user_out, item_out) = refs[:n_user], refs[n_user:-2], refs[-2:]
    for smooth, own, parts, out in (
        (user_smooth, user_own, user_parts, user_out),
        (item_smooth, item_own, item_parts, item_out),
    ):
        total = own[...]
        for part in parts:
            total = total + decode(part)
        out[...] = DATA_SCALE * total + smooth[...]


def swap(array, axis, size, mask):
    return lax.ppermute(array, axis, [(i, i ^ mask) for i in range(size)])


def local(
    n_row, n_col,
    user_factors, item_factors, ratings, tile_cell, keep_count, send_count, user_nbrs, item_nbrs
):
    f32, bf16, i16 = jnp.float32, jnp.bfloat16, jnp.int16
    user_own, item_own = user_factors, item_factors[0]
    user_rows, rank = user_own.shape
    item_rows = item_own.shape[0]
    block_users, block_items = user_rows * n_col, item_rows * n_row
    knn = user_nbrs.shape[1]
    direct = n_col == 8 and n_row == 4

    if direct:
        item_in = [item_own] + [swap(item_own, "row", n_row, k) for k in range(1, n_row)]
        even = [user_own] + [swap(user_own, "col", n_col, k) for k in range(2, n_col, 2)]
        odd = [swap(part, "col", n_col, 1) for part in even]
        user_in = [part for pair in zip(even, odd) for part in pair]
    else:
        item_in = [lax.all_gather(item_own, "row", axis=0, tiled=True)]
        user_in = [lax.all_gather(user_own, "col", axis=0, tiled=True)]

    user_adj, item_adj = call(
        adjacency_kernel,
        [struct(user_rows, block_users, bf16), struct(item_rows, block_items, bf16)],
        [user_nbrs, item_nbrs[0]],
        "adjacency",
        flops=2 * knn * (user_rows * block_users + item_rows * block_items),
        nbytes=2 * (user_rows * block_users + item_rows * block_items),
    )

    if direct:
        outs = [
            struct(block_users // 2, rank, f32),
            struct(block_users // 2, rank, f32),
            struct(item_rows, rank, f32),
        ] + [struct(item_rows + EXTRA, rank, i16)] * (n_row - 1)
    else:
        outs = [struct(block_users, rank, f32), struct(block_items, rank, f32)]
    grads = call(
        functools.partial(main_kernel, len(user_in), len(item_in), direct),
        outs,
        [keep_count, send_count, tile_cell, ratings[0, 0]] + user_in + item_in,
        "tiles",
        scratch=[
            pltpu.VMEM((block_users, rank), bf16),
            pltpu.VMEM((block_items, rank), bf16),
            pltpu.VMEM((block_users, rank), f32),
            pltpu.VMEM((block_items, rank), f32),
        ],
        flops=6 * ratings.shape[2] * 128 * 128 * 128,
        nbytes=ratings.size * 2,
        smem=3,
        limit=24,
    )

    smooth = call(
        functools.partial(smooth_kernel, len(user_in), len(item_in)),
        [struct(user_rows, rank, f32), struct(item_rows, rank, f32)],
        [user_adj, item_adj, user_own, item_own] + user_in + item_in,
        "smooth",
        scratch=[pltpu.VMEM((block_users, rank), bf16), pltpu.VMEM((block_items, rank), bf16)],
        flops=2 * rank * (user_rows * block_users + item_rows * block_items),
        nbytes=4 * (user_rows * block_users + item_rows * block_items),
    )

    if direct:
        user_keep, user_send, item_total, *item_send = grads
        user_recv = swap(user_send, "col", n_col, 1)
        item_parts = [swap(part, "row", n_row, k) for k, part in enumerate(item_send, 1)]
        user_total, *chip_send = call(
            chip_sum_kernel,
            [struct(user_rows, rank, f32)]
            + [struct(user_rows + EXTRA, rank, i16)] * (n_col // 2 - 1),
            [user_keep, user_recv],
            "chip_sum",
            flops=block_users * rank,
            nbytes=6 * block_users * rank,
        )
        user_parts = [swap(part, "col", n_col, 2 * k) for k, part in enumerate(chip_send, 1)]
    else:
        user_total = lax.psum_scatter(grads[0], "col", scatter_dimension=0, tiled=True)
        item_total = lax.psum_scatter(grads[1], "row", scatter_dimension=0, tiled=True)
        user_parts, item_parts = [], []

    grad_users, grad_items = call(
        functools.partial(final_kernel, len(user_parts)),
        [struct(user_rows, rank, f32), struct(item_rows, rank, f32)],
        list(smooth) + [user_total, item_total] + user_parts + item_parts,
        "finish",
        flops=8 * (user_rows + item_rows) * rank,
        nbytes=20 * (user_rows + item_rows) * rank,
    )
    return (grad_users, grad_items[None])


def solution(mesh):
    placed = (
        P(("row", "col"), None),
        P("col", "row", None),
        P("row", "col", None, None, None),
        P("row", "col", None),
        P("row", "col"),
        P("row", "col", None),
        P(("row", "col"), None),
        P("col", "row", None),
    )
    return jax.shard_map(
        functools.partial(local, mesh.shape["row"], mesh.shape["col"]),
        mesh=mesh,
        in_specs=placed,
        out_specs=(P(("row", "col"), None), P("col", "row", None)),
        check_vma=False,
    )
```

```python
import functools

import jax
import jax.numpy as jnp
from jax import lax
from jax.experimental import pallas as pl
from jax.experimental.pallas import tpu as pltpu
from jax.sharding import PartitionSpec as P

ALPHA = 0.5
DATA_SCALE = 0.0625
SMOOTH = 4.0
GROUP = 4
COST_NEAR = 10**10
COST_IF = 0
COST_IL = 10**10
VMEM = pl.BlockSpec(memory_space=pltpu.VMEM)
ANY = pl.BlockSpec(memory_space=pl.ANY)
HBM = pl.BlockSpec(memory_space=pltpu.HBM)


def call(kernel, outs, ins, name, spaces=None, scratch=(), flops=0, nbytes=0, limit=16):
    return pl.pallas_call(
        kernel,
        out_shape=outs,
        in_specs=spaces or [VMEM] * len(ins),
        out_specs=jax.tree.map(lambda _: VMEM, outs),
        scratch_shapes=scratch,
        cost_estimate=pl.CostEstimate(flops=flops, bytes_accessed=nbytes, transcendentals=0),
        compiler_params=pltpu.CompilerParams(vmem_limit_bytes=limit * 2**20),
        name=name,
    )(*ins)


def struct(rows, cols, dtype):
    return jax.ShapeDtypeStruct((rows, cols), dtype)


EXTRA = 16
OCTAVE = 64.0
TOP = 32400.0


def encode(block, out_ref, start):
    rows = block.shape[0]
    top = jnp.max(jnp.abs(block), axis=0, keepdims=True)
    level = jnp.ceil(jnp.log2(jnp.maximum(top, 1e-30)) * OCTAVE)
    fixed = jnp.round(block * (jnp.exp2(level * (-1.0 / OCTAVE)) * TOP))
    out_ref[start : start + rows, :] = fixed.astype(jnp.int32).astype(jnp.int16)
    spread = jnp.broadcast_to(level, (EXTRA, block.shape[1]))
    out_ref[start + rows : start + rows + EXTRA, :] = spread.astype(jnp.int32).astype(jnp.int16)


def decode(ref, start, rows):
    stop = start + rows
    level = ref[stop : stop + EXTRA, :].astype(jnp.int32).astype(jnp.float32)[:1]
    scale = jnp.exp2(level * (1.0 / OCTAVE)) * (1.0 / TOP)
    return ref[start:stop, :].astype(jnp.int32).astype(jnp.float32) * scale


def counts_of(nbrs, adj):
    count, width = nbrs.shape
    blocks = adj.shape[0] // 128
    bits = count.bit_length()
    fields = 31 // bits
    words = -(-blocks // fields)
    step = 16
    for left in range(0, width, 128):
        lanes = slice(left, min(left + 128, width))
        span = lanes.stop - lanes.start

        def body(turn, _, lanes=lanes, span=span):
            here = turn * step + lax.broadcasted_iota(jnp.int32, (step, span), 0)
            totals = [jnp.zeros((step, span), jnp.int32)] * words
            for k in range(count):
                index = nbrs[k : k + 1, lanes]
                block = index >> 7
                hit = jnp.broadcast_to(index & 127, (step, span)) == here
                for word in range(words):
                    field = block - word * fields
                    inside = (field >= 0) & (field < fields)
                    one = jnp.where(inside, 1 << (jnp.where(inside, field, 0) * bits), 0)
                    one = jnp.broadcast_to(one, (step, span))
                    totals[word] = totals[word] + jnp.where(hit, one, 0)
            for block in range(blocks):
                word, field = divmod(block, fields)
                value = (totals[word] >> (field * bits)) & ((1 << bits) - 1)
                at = pl.ds(pl.multiple_of(block * 128 + turn * step, step), step)
                adj[at, lanes] = value.astype(jnp.float32).astype(jnp.bfloat16)
            return 0

        lax.fori_loop(0, 128 // step, body, 0)


def stage_kernel(
    user_nbrs, item_nbrs, ratings, user_adj, item_adj, held, user_held, item_held, sem
):
    copies = [
        pltpu.make_async_copy(src, dst, sem.at[k])
        for k, (src, dst) in enumerate(
            ((user_nbrs, user_held), (item_nbrs, item_held), (ratings, held))
        )
    ]
    for copy in copies:
        copy.start()
    copies[0].wait()
    counts_of(user_held, user_adj)
    copies[1].wait()
    counts_of(item_held, item_adj)
    copies[2].wait()


def pair_kernel(user_own, item_own, user_other, item_other, user_out, item_out, sem):
    copies = []
    for k, (own, other, out) in enumerate(
        ((user_own, user_other, user_out), (item_own, item_other, item_out))
    ):
        rows = own.shape[0]
        copies.append(pltpu.make_async_copy(own, out.at[:rows, :], sem.at[k]))
        copies[-1].start()
        out[rows:, :] = other[...]
    for copy in copies:
        copy.wait()


def tie_kernel(source, out):
    out[...] = source[...]


def col_masks():
    me = lax.axis_index("col")
    first = 2 + 2 * (me & 1)
    return me, first, 6 - first


def place(user_in, item_in, users, items):
    if len(user_in) == 1:
        users[...] = user_in[0][...]
        items[...] = item_in[0][...]
        return
    pair, second, swap_pair, swap_second = user_in
    me, first, other = col_masks()
    rows = pair.shape[0] // 2
    for ref, masks in (
        (pair, (0, first)),
        (second, (other, 6)),
        (swap_pair, (1, other ^ 1)),
        (swap_second, (first ^ 1, 7)),
    ):
        for k, mask in enumerate(masks):
            at = pl.ds(pl.multiple_of((me ^ mask) * rows, rows), rows)
            users[at, :] = ref[k * rows : (k + 1) * rows, :]
    me = lax.axis_index("row")
    rows = item_in[0].shape[0] // 2
    for ref, masks in zip(item_in, ((0, 2), (1, 3))):
        for k, mask in enumerate(masks):
            at = pl.ds(pl.multiple_of((me ^ mask) * rows, rows), rows)
            items[at, :] = ref[k * rows : (k + 1) * rows, :]


def main_kernel(n_user, n_item, direct, keep_in, sends_in, cells_in, ratings, *refs):
    user_in, refs = refs[:n_user], refs[n_user:]
    item_in, refs = refs[:n_item], refs[n_item + 2 :]
    outs, (keep, sends, cells, users, items, user_acc, item_acc, sem) = refs[:-8], refs[-8:]
    tile = ratings.shape[1]
    item_count = items.shape[0] // tile
    copies = [
        pltpu.make_async_copy(src, dst, sem.at[k])
        for k, (src, dst) in enumerate(((keep_in, keep), (sends_in, sends), (cells_in, cells)))
    ]
    for copy in copies:
        copy.start()
    place(user_in, item_in, users, items)
    user_acc[...] = jnp.zeros_like(user_acc)
    item_acc[...] = jnp.zeros_like(item_acc)
    for copy in copies:
        copy.wait()
    live = keep[0, 0]
    for q in range(sends.shape[2]):
        live = live + sends[0, 0, q]

    def body(turn, _):
        work = []
        for g in range(GROUP):
            slot = turn * GROUP + g
            cell = cells[0, 0, slot]
            upper = cell // item_count
            lower = cell - upper * item_count
            user_at = pl.ds(pl.multiple_of(upper * tile, tile), tile)
            item_at = pl.ds(pl.multiple_of(lower * tile, tile), tile)
            left = users[user_at, :]
            right = items[item_at, :]
            product = lax.dot_general(
                left, right, (((1,), (1,)), ((), ())), preferred_element_type=jnp.float32
            )
            value = ratings[slot].astype(jnp.float32)
            error = (1.0 + ALPHA * value) * (product - jnp.where(value > 0, 1.0, 0.0))
            error = jnp.where(slot < live, error, 0.0).astype(jnp.bfloat16)
            work.append((user_at, item_at, left, right, error))
        for user_at, item_at, left, right, error in work:
            user_acc[user_at, :] += jnp.dot(error, right, preferred_element_type=jnp.float32)
            item_acc[item_at, :] += lax.dot_general(
                error, left, (((0,), (0,)), ((), ())), preferred_element_type=jnp.float32
            )
        return 0

    lax.fori_loop(0, (live + GROUP - 1) // GROUP, body, 0)

    if not direct:
        outs[0][...] = user_acc[...]
        outs[1][...] = item_acc[...]
        return
    user_keep, user_send, item_keep, item_send = outs
    me, first, other = col_masks()
    rows = user_keep.shape[0] // 4
    for k, (mine, yours) in enumerate(((0, 1), (other, first ^ 1), (first, other ^ 1), (6, 7))):
        for out, mask in ((user_keep, mine), (user_send, yours)):
            at = pl.ds(pl.multiple_of((me ^ mask) * rows, rows), rows)
            out[k * rows : (k + 1) * rows, :] = user_acc[at, :]
    me = lax.axis_index("row")
    rows = item_keep.shape[0] // 2
    for k, (mine, yours) in enumerate(((0, 1), (2, 3))):
        at = pl.ds(pl.multiple_of((me ^ mine) * rows, rows), rows)
        item_keep[k * rows : (k + 1) * rows, :] = item_acc[at, :]
        at = pl.ds(pl.multiple_of((me ^ yours) * rows, rows), rows)
        encode(item_acc[at, :], item_send, k * (rows + EXTRA))


def chip_sum_kernel(keep, recv, total, send):
    rows = total.shape[0] // 2
    total[...] = keep[: 2 * rows, :] + recv[: 2 * rows, :]
    for k in range(2):
        at = slice((k + 2) * rows, (k + 3) * rows)
        encode(keep[at, :] + recv[at, :], send, k * (rows + EXTRA))


def fold_kernel(keep, recv, total, send):
    rows = total.shape[0]
    total[...] = keep[:rows, :] + decode(recv, 0, rows)
    encode(keep[rows:, :] + decode(recv, rows + EXTRA, rows), send, 0)


def smooth_kernel(n_user, n_item, user_adj, item_adj, *refs):
    user_in, refs = refs[:n_user], refs[n_user:]
    item_in, refs = refs[:n_item], refs[n_item:]
    user_own, item_own, user_out, item_out, users, items = refs
    place(user_in, item_in, users, items)
    for adj, whole, own, out in (
        (user_adj, users, user_own, user_out),
        (item_adj, items, item_own, item_out),
    ):
        near = lax.dot_general(
            whole[...], adj[...], (((0,), (0,)), ((), ())), preferred_element_type=jnp.float32
        )
        mine = own[: out.shape[0], :].astype(jnp.float32)
        out[...] = SMOOTH * (mine - near.T * (1.0 / 16))


def final_kernel(user_smooth, item_smooth, user_total, item_total, *refs):
    user_out, item_out = refs[-2:]
    parts = refs[:-2] or (None, None)
    for smooth, total, part, out in (
        (user_smooth, user_total, parts[0], user_out),
        (item_smooth, item_total, parts[1], item_out),
    ):
        whole = total[...]
        if part is not None:
            whole = whole + decode(part, 0, whole.shape[0])
        out[...] = DATA_SCALE * whole + smooth[...]


def swap(array, axis, size, even, odd=None):
    odd = even if odd is None else odd
    return lax.ppermute(array, axis, [(i, i ^ (odd if i % 2 else even)) for i in range(size)])


def local(
    n_row, n_col,
    user_factors, item_factors, ratings, tile_cell, keep_count, send_count, user_nbrs, item_nbrs
):
    f32, bf16, i16 = jnp.float32, jnp.bfloat16, jnp.int16
    user_own, item_own = user_factors, item_factors[0]
    user_rows, rank = user_own.shape
    item_rows = item_own.shape[0]
    block_users, block_items = user_rows * n_col, item_rows * n_row
    pin = lambda array: pltpu.with_memory_space_constraint(array, pltpu.HBM)
    knn = user_nbrs.shape[1]
    slots, tile = ratings.shape[2:4]
    direct = n_col == 8 and n_row == 4

    if direct:
        first = swap(user_own, "col", n_col, 2, 4)
        far = swap(item_own, "row", n_row, 2)
        user_pair, item_pair = call(
            pair_kernel,
            [struct(2 * user_rows, rank, bf16), struct(2 * item_rows, rank, bf16)],
            [pin(user_own), pin(item_own), first, far],
            "pair",
            spaces=[HBM, HBM, VMEM, VMEM],
            scratch=[pltpu.SemaphoreType.DMA((2,))],
            nbytes=8 * user_rows * rank,
        )
        second = swap(user_pair, "col", n_col, 4, 2)
        near = swap(item_pair, "row", n_row, 1)
        near = call(
            tie_kernel, struct(2 * item_rows, rank, bf16), [near], "tie", flops=COST_NEAR
        )
        swaps = [swap(user_pair, "col", n_col, 1), swap(second, "col", n_col, 1)]
        user_in = [user_pair, second] + swaps
        item_in = [item_pair, near]
    else:
        item_in = [lax.all_gather(item_own, "row", axis=0, tiled=True)]
        user_in = [lax.all_gather(user_own, "col", axis=0, tiled=True)]

    user_adj, item_adj, held = call(
        stage_kernel,
        [
            struct(block_users, user_rows, bf16),
            struct(block_items, item_rows, bf16),
            jax.ShapeDtypeStruct((slots, tile, tile), bf16),
        ],
        [pin(user_nbrs.T), pin(item_nbrs[0].T), pin(ratings[0, 0])],
        "stage",
        spaces=[HBM] * 3,
        scratch=[
            pltpu.VMEM((knn, user_rows), jnp.int32),
            pltpu.VMEM((knn, item_rows), jnp.int32),
            pltpu.SemaphoreType.DMA((3,)),
        ],
        flops=2 * knn * (user_rows * block_users + item_rows * block_items),
        nbytes=ratings.size * 2,
    )

    if direct:
        outs = [
            struct(block_users // 2, rank, f32),
            struct(block_users // 2, rank, f32),
            struct(block_items // 2, rank, f32),
            struct(block_items // 2 + 2 * EXTRA, rank, i16),
        ]
    else:
        outs = [struct(block_users, rank, f32), struct(block_items, rank, f32)]
    n_user, n_item = len(user_in), len(item_in)
    grads = call(
        functools.partial(main_kernel, n_user, n_item, direct),
        outs,
        [keep_count, send_count, tile_cell, held] + user_in + item_in + [user_adj, item_adj],
        "tiles",
        spaces=[HBM] * 3 + [VMEM] * (1 + n_user + n_item) + [ANY] * 2,
        scratch=[
            pltpu.SMEM(keep_count.shape, jnp.int32),
            pltpu.SMEM(send_count.shape, jnp.int32),
            pltpu.SMEM(tile_cell.shape, jnp.int32),
            pltpu.VMEM((block_users, rank), bf16),
            pltpu.VMEM((block_items, rank), bf16),
            pltpu.VMEM((block_users, rank), f32),
            pltpu.VMEM((block_items, rank), f32),
            pltpu.SemaphoreType.DMA((3,)),
        ],
        flops=6 * slots * tile * tile * rank,
        nbytes=ratings.size * 2,
        limit=24,
    )

    own = [user_in[0], item_in[0]] if direct else [user_own, item_own]
    smooth = call(
        functools.partial(smooth_kernel, n_user, n_item),
        [struct(user_rows, rank, f32), struct(item_rows, rank, f32)],
        [user_adj, item_adj] + user_in + item_in + own,
        "smooth",
        scratch=[pltpu.VMEM((block_users, rank), bf16), pltpu.VMEM((block_items, rank), bf16)],
        flops=2 * rank * (user_rows * block_users + item_rows * block_items),
        nbytes=4 * (user_rows * block_users + item_rows * block_items),
    )

    if direct:
        user_keep, user_send, item_keep, item_send = grads
        user_recv = swap(user_send, "col", n_col, 1)
        item_recv = swap(item_send, "row", n_row, 1)
        item_total, item_last = call(
            fold_kernel,
            [struct(item_rows, rank, f32), struct(item_rows + EXTRA, rank, i16)],
            [item_keep, item_recv],
            "item_fold",
            flops=COST_IF,
        )
        item_last = swap(item_last, "row", n_row, 2)
        item_last = call(
            tie_kernel, struct(item_rows + EXTRA, rank, i16), [item_last], "tie", flops=COST_IL
        )
        pair_sum, chip_send = call(
            chip_sum_kernel,
            [struct(2 * user_rows, rank, f32), struct(2 * (user_rows + EXTRA), rank, i16)],
            [user_keep, user_recv],
            "chip_sum",
        )
        chip_recv = swap(chip_send, "col", n_col, 2, 4)
        user_total, user_last = call(
            fold_kernel,
            [struct(user_rows, rank, f32), struct(user_rows + EXTRA, rank, i16)],
            [pair_sum, chip_recv],
            "user_fold",
            flops=4 * user_rows * rank,
            nbytes=16 * user_rows * rank,
        )
        parts = [swap(user_last, "col", n_col, 4, 2), item_last]
    else:
        user_total = lax.psum_scatter(grads[0], "col", scatter_dimension=0, tiled=True)
        item_total = lax.psum_scatter(grads[1], "row", scatter_dimension=0, tiled=True)
        parts = []

    grad_users, grad_items = call(
        final_kernel,
        [struct(user_rows, rank, f32), struct(item_rows, rank, f32)],
        list(smooth) + [user_total, item_total] + parts,
        "finish",
        flops=8 * (user_rows + item_rows) * rank,
        nbytes=20 * (user_rows + item_rows) * rank,
    )
    return (grad_users, grad_items[None])


def solution(mesh):
    placed = (
        P(("row", "col"), None),
        P("col", "row", None),
        P("row", "col", None, None, None),
        P("row", "col", None),
        P("row", "col"),
        P("row", "col", None),
        P(("row", "col"), None),
        P("col", "row", None),
    )
    return jax.shard_map(
        functools.partial(local, mesh.shape["row"], mesh.shape["col"]),
        mesh=mesh,
        in_specs=placed,
        out_specs=(P(("row", "col"), None), P("col", "row", None)),
        check_vma=False,
    )
```

```python
import functools

import jax
import jax.numpy as jnp
from jax import lax
from jax.experimental import pallas as pl
from jax.experimental.pallas import tpu as pltpu
from jax.sharding import PartitionSpec as P

ALPHA = 0.5
DATA_SCALE = 0.0625
SMOOTH = 4.0
GROUP = 12
COST_NEAR = 10**10
COST_AC = 0
COST_BE = 0
COST_STAGE = 0
COST_SMOOTH = 0
COST_IF = 0
COST_IL = 10**10
VMEM = pl.BlockSpec(memory_space=pltpu.VMEM)
ANY = pl.BlockSpec(memory_space=pl.ANY)
HBM = pl.BlockSpec(memory_space=pltpu.HBM)


def call(kernel, outs, ins, name, spaces=None, scratch=(), flops=0, nbytes=0, limit=16):
    return pl.pallas_call(
        kernel,
        out_shape=outs,
        in_specs=spaces or [VMEM] * len(ins),
        out_specs=jax.tree.map(lambda _: VMEM, outs),
        scratch_shapes=scratch,
        cost_estimate=pl.CostEstimate(flops=flops, bytes_accessed=nbytes, transcendentals=0),
        compiler_params=pltpu.CompilerParams(vmem_limit_bytes=limit * 2**20),
        name=name,
    )(*ins)


def struct(rows, cols, dtype):
    return jax.ShapeDtypeStruct((rows, cols), dtype)


EXTRA = 16
OCTAVE = 64.0
TOP = 32400.0


def encode(block, out_ref, start):
    rows = block.shape[0]
    top = jnp.max(jnp.abs(block), axis=0, keepdims=True)
    level = jnp.ceil(jnp.log2(jnp.maximum(top, 1e-30)) * OCTAVE)
    fixed = jnp.round(block * (jnp.exp2(level * (-1.0 / OCTAVE)) * TOP))
    out_ref[start : start + rows, :] = fixed.astype(jnp.int32).astype(jnp.int16)
    spread = jnp.broadcast_to(level, (EXTRA, block.shape[1]))
    out_ref[start + rows : start + rows + EXTRA, :] = spread.astype(jnp.int32).astype(jnp.int16)


def decode(ref, start, rows):
    stop = start + rows
    level = ref[stop : stop + EXTRA, :].astype(jnp.int32).astype(jnp.float32)[:1]
    scale = jnp.exp2(level * (1.0 / OCTAVE)) * (1.0 / TOP)
    return ref[start:stop, :].astype(jnp.int32).astype(jnp.float32) * scale


def counts_of(nbrs, adj, digits):
    count, width = nbrs.shape
    blocks = adj.shape[0] // 128
    bits = count.bit_length()
    fields = 31 // bits
    words = -(-blocks // fields)
    step = 32
    index = nbrs[...]
    block = index >> 7
    digits[0] = index & 127
    for word in range(words):
        field = block - word * fields
        inside = (field >= 0) & (field < fields)
        digits[1 + word] = jnp.where(inside, 1 << (jnp.where(inside, field, 0) * bits), 0)
    for left in range(0, width, 128):
        lanes = slice(left, min(left + 128, width))
        span = lanes.stop - lanes.start

        def body(turn, _, lanes=lanes, span=span):
            here = turn * step + lax.broadcasted_iota(jnp.int32, (step, span), 0)
            totals = [jnp.zeros((step, span), jnp.int32)] * words
            for k in range(count):
                hit = jnp.broadcast_to(digits[0, k : k + 1, lanes], (step, span)) == here
                for word in range(words):
                    one = jnp.broadcast_to(digits[1 + word, k : k + 1, lanes], (step, span))
                    totals[word] = totals[word] + jnp.where(hit, one, 0)
            for block in range(blocks):
                word, field = divmod(block, fields)
                value = (totals[word] >> (field * bits)) & ((1 << bits) - 1)
                at = pl.ds(pl.multiple_of(block * 128 + turn * step, step), step)
                adj[at, lanes] = value.astype(jnp.float32).astype(jnp.bfloat16)
            return 0

        lax.fori_loop(0, 128 // step, body, 0)


def words_of(count, rows):
    return 1 + -(-(rows // 128) // (31 // count.bit_length()))


def stage_kernel(nbrs, ratings, adj, held, near, digits, sem):
    copies = [
        pltpu.make_async_copy(nbrs, near, sem.at[0]),
        pltpu.make_async_copy(ratings, held, sem.at[1]),
    ]
    for copy in copies:
        copy.start()
    copies[0].wait()
    counts_of(near, adj, digits)
    copies[1].wait()


def user_pair_kernel(own, other, item_own, out, item_held, sem):
    rows = own.shape[0]
    copies = [
        pltpu.make_async_copy(own, out.at[:rows, :], sem.at[0]),
        pltpu.make_async_copy(item_own, item_held, sem.at[1]),
    ]
    for copy in copies:
        copy.start()
    out[rows:, :] = other[...]
    for copy in copies:
        copy.wait()


def pair_kernel(own, other, out):
    rows = own.shape[0]
    out[:rows, :] = own[...]
    out[rows:, :] = other[...]


def tie_kernel(source, *refs):
    refs[-1][...] = source[...]


def tie(array, cost, after=None):
    if not cost:
        return array
    later = [] if after is None else [after]
    return call(
        tie_kernel,
        struct(*array.shape, array.dtype),
        [array] + later,
        "tie",
        spaces=[VMEM] + [ANY] * len(later),
        flops=cost,
    )


def col_masks():
    me = lax.axis_index("col")
    first = 2 + 2 * (me & 1)
    return me, first, 6 - first


def place(user_in, item_in, users, items):
    if len(user_in) == 1:
        users[...] = user_in[0][...]
        items[...] = item_in[0][...]
        return
    pair, second, swap_pair, swap_second = user_in
    me, first, other = col_masks()
    rows = pair.shape[0] // 2
    for ref, masks in (
        (pair, (0, first)),
        (second, (other, 6)),
        (swap_pair, (1, other ^ 1)),
        (swap_second, (first ^ 1, 7)),
    ):
        for k, mask in enumerate(masks):
            at = pl.ds(pl.multiple_of((me ^ mask) * rows, rows), rows)
            users[at, :] = ref[k * rows : (k + 1) * rows, :]
    me = lax.axis_index("row")
    rows = item_in[0].shape[0] // 2
    for ref, masks in zip(item_in, ((0, 2), (1, 3))):
        for k, mask in enumerate(masks):
            at = pl.ds(pl.multiple_of((me ^ mask) * rows, rows), rows)
            items[at, :] = ref[k * rows : (k + 1) * rows, :]


def main_kernel(n_user, n_item, direct, keep_in, sends_in, cells_in, ratings, *refs):
    user_in, refs = refs[:n_user], refs[n_user:]
    item_in, refs = refs[:n_item], refs[n_item:]
    outs, (keep, sends, cells, users, items, user_acc, item_acc, sem) = refs[:-8], refs[-8:]
    slots, tile = ratings.shape[:2]
    group = max(g for g in range(1, GROUP + 1) if slots % g == 0)
    item_count = items.shape[0] // tile
    copies = [
        pltpu.make_async_copy(src, dst, sem.at[k])
        for k, (src, dst) in enumerate(((keep_in, keep), (sends_in, sends), (cells_in, cells)))
    ]
    for copy in copies:
        copy.start()
    place(user_in, item_in, users, items)
    user_acc[...] = jnp.zeros_like(user_acc)
    item_acc[...] = jnp.zeros_like(item_acc)
    for copy in copies:
        copy.wait()
    live = keep[0, 0]
    for q in range(sends.shape[2]):
        live = live + sends[0, 0, q]

    def body(turn, _):
        work = []
        for g in range(group):
            slot = turn * group + g
            cell = cells[0, 0, slot]
            upper = cell // item_count
            lower = cell - upper * item_count
            user_at = pl.ds(pl.multiple_of(upper * tile, tile), tile)
            item_at = pl.ds(pl.multiple_of(lower * tile, tile), tile)
            left = users[user_at, :]
            right = items[item_at, :]
            product = lax.dot_general(
                left, right, (((1,), (1,)), ((), ())), preferred_element_type=jnp.float32
            )
            value = ratings[slot].astype(jnp.float32)
            error = (1.0 + ALPHA * value) * (product - jnp.where(value > 0, 1.0, 0.0))
            error = jnp.where(slot < live, error, 0.0).astype(jnp.bfloat16)
            work.append((user_at, item_at, left, right, error))
        for user_at, item_at, left, right, error in work:
            user_acc[user_at, :] += jnp.dot(error, right, preferred_element_type=jnp.float32)
            item_acc[item_at, :] += lax.dot_general(
                error, left, (((0,), (0,)), ((), ())), preferred_element_type=jnp.float32
            )
        return 0

    lax.fori_loop(0, (live + group - 1) // group, body, 0)

    if not direct:
        outs[0][...] = user_acc[...]
        outs[1][...] = item_acc[...]
        return
    user_keep, user_send, item_keep, item_send = outs
    me, first, other = col_masks()
    rows = user_keep.shape[0] // 4
    for k, (mine, yours) in enumerate(((0, 1), (other, first ^ 1), (first, other ^ 1), (6, 7))):
        for out, mask in ((user_keep, mine), (user_send, yours)):
            at = pl.ds(pl.multiple_of((me ^ mask) * rows, rows), rows)
            out[k * rows : (k + 1) * rows, :] = user_acc[at, :]
    me = lax.axis_index("row")
    rows = item_keep.shape[0] // 2
    for k, (mine, yours) in enumerate(((0, 1), (2, 3))):
        at = pl.ds(pl.multiple_of((me ^ mine) * rows, rows), rows)
        item_keep[k * rows : (k + 1) * rows, :] = item_acc[at, :]
        at = pl.ds(pl.multiple_of((me ^ yours) * rows, rows), rows)
        encode(item_acc[at, :], item_send, k * (rows + EXTRA))


def chip_sum_kernel(keep, recv, total, send):
    rows = total.shape[0] // 2
    total[...] = keep[: 2 * rows, :] + recv[: 2 * rows, :]
    for k in range(2):
        at = slice((k + 2) * rows, (k + 3) * rows)
        encode(keep[at, :] + recv[at, :], send, k * (rows + EXTRA))


def fold_kernel(keep, recv, total, send):
    rows = total.shape[0]
    total[...] = keep[:rows, :] + decode(recv, 0, rows)
    encode(keep[rows:, :] + decode(recv, rows + EXTRA, rows), send, 0)


def smooth_kernel(n_user, n_item, user_nbrs, item_adj, *refs):
    user_in, refs = refs[:n_user], refs[n_user:]
    item_in, refs = refs[:n_item], refs[n_item:]
    user_own, item_own, _, user_out, item_out, users, items, near, user_adj, digits, sem = refs
    copy = pltpu.make_async_copy(user_nbrs, near, sem)
    copy.start()
    place(user_in, item_in, users, items)
    copy.wait()
    counts_of(near, user_adj, digits)
    for adj, whole, own, out in (
        (user_adj, users, user_own, user_out),
        (item_adj, items, item_own, item_out),
    ):
        near = lax.dot_general(
            whole[...], adj[...], (((0,), (0,)), ((), ())), preferred_element_type=jnp.float32
        )
        mine = own[: out.shape[0], :].astype(jnp.float32)
        out[...] = SMOOTH * (mine - near.T * (1.0 / 16))


def final_kernel(user_smooth, item_smooth, user_total, item_total, *refs):
    user_out, item_out = refs[-2:]
    parts = refs[:-2] or (None, None)
    for smooth, total, part, out in (
        (user_smooth, user_total, parts[0], user_out),
        (item_smooth, item_total, parts[1], item_out),
    ):
        whole = total[...]
        if part is not None:
            whole = whole + decode(part, 0, whole.shape[0])
        out[...] = DATA_SCALE * whole + smooth[...]


def swap(array, axis, size, even, odd=None):
    odd = even if odd is None else odd
    return lax.ppermute(array, axis, [(i, i ^ (odd if i % 2 else even)) for i in range(size)])


def local(
    n_row, n_col,
    user_factors, item_factors, ratings, tile_cell, keep_count, send_count, user_nbrs, item_nbrs
):
    f32, bf16, i16 = jnp.float32, jnp.bfloat16, jnp.int16
    user_own, item_own = user_factors, item_factors[0]
    user_rows, rank = user_own.shape
    item_rows = item_own.shape[0]
    block_users, block_items = user_rows * n_col, item_rows * n_row
    pin = lambda array: pltpu.with_memory_space_constraint(array, pltpu.HBM)
    knn = user_nbrs.shape[1]
    slots, tile = ratings.shape[2:4]
    direct = n_col == 8 and n_row == 4

    if direct:
        far = swap(item_own, "row", n_row, 2)
        first = swap(user_own, "col", n_col, 2, 4)
        user_pair, item_held = call(
            user_pair_kernel,
            [struct(2 * user_rows, rank, bf16), struct(item_rows, rank, bf16)],
            [pin(user_own), first, pin(item_own)],
            "user_pair",
            spaces=[HBM, VMEM, HBM],
            scratch=[pltpu.SemaphoreType.DMA((2,))],
        )
        second = tie(swap(user_pair, "col", n_col, 4, 2), COST_BE)
        item_pair = call(
            pair_kernel,
            struct(2 * item_rows, rank, bf16),
            [item_held, far],
            "item_pair",
        )
        near = swap(item_pair, "row", n_row, 1)
        near = tie(near, COST_NEAR)
        user_in = [user_pair, second, swap(user_pair, "col", n_col, 1), swap(second, "col", n_col, 1)]
        item_in = [item_pair, near]
    else:
        item_in = [lax.all_gather(item_own, "row", axis=0, tiled=True)]
        user_in = [lax.all_gather(user_own, "col", axis=0, tiled=True)]

    item_adj, held = call(
        stage_kernel,
        [
            struct(block_items, item_rows, bf16),
            jax.ShapeDtypeStruct((slots, tile, tile), bf16),
        ],
        [pin(item_nbrs[0].T), pin(ratings[0, 0])],
        "stage",
        spaces=[HBM] * 2,
        scratch=[
            pltpu.VMEM((knn, item_rows), jnp.int32),
            pltpu.VMEM((words_of(knn, block_items), knn, item_rows), jnp.int32),
            pltpu.SemaphoreType.DMA((2,)),
        ],
        flops=COST_STAGE,
    )
    if direct:
        outs = [
            struct(block_users // 2, rank, f32),
            struct(block_users // 2, rank, f32),
            struct(block_items // 2, rank, f32),
            struct(block_items // 2 + 2 * EXTRA, rank, i16),
        ]
    else:
        outs = [struct(block_users, rank, f32), struct(block_items, rank, f32)]
    n_user, n_item = len(user_in), len(item_in)
    grads = call(
        functools.partial(main_kernel, n_user, n_item, direct),
        outs,
        [keep_count, send_count, tile_cell, held] + user_in + item_in,
        "tiles",
        spaces=[HBM] * 3 + [VMEM] * (1 + n_user + n_item),
        scratch=[
            pltpu.SMEM(keep_count.shape, jnp.int32),
            pltpu.SMEM(send_count.shape, jnp.int32),
            pltpu.SMEM(tile_cell.shape, jnp.int32),
            pltpu.VMEM((block_users, rank), bf16),
            pltpu.VMEM((block_items, rank), bf16),
            pltpu.VMEM((block_users, rank), f32),
            pltpu.VMEM((block_items, rank), f32),
            pltpu.SemaphoreType.DMA((3,)),
        ],
        flops=6 * slots * tile * tile * rank,
        nbytes=ratings.size * 2,
        limit=24,
    )

    if direct:
        user_keep, user_send, item_keep, item_send = grads
        user_recv = swap(user_send, "col", n_col, 1)
        item_recv = swap(item_send, "row", n_row, 1)
        item_total, item_last = call(
            fold_kernel,
            [struct(item_rows, rank, f32), struct(item_rows + EXTRA, rank, i16)],
            [item_keep, item_recv],
            "item_fold",
            flops=COST_IF,
        )
        item_last = swap(item_last, "row", n_row, 2)
        pair_sum, chip_send = call(
            chip_sum_kernel,
            [struct(2 * user_rows, rank, f32), struct(2 * (user_rows + EXTRA), rank, i16)],
            [user_keep, user_recv],
            "chip_sum",
        )
        chip_recv = swap(chip_send, "col", n_col, 2, 4)
        user_total, user_last = call(
            fold_kernel,
            [struct(user_rows, rank, f32), struct(user_rows + EXTRA, rank, i16)],
            [pair_sum, chip_recv],
            "user_fold",
            flops=4 * user_rows * rank,
            nbytes=16 * user_rows * rank,
        )
        parts = [swap(user_last, "col", n_col, 4, 2), item_last]
    else:
        user_total = lax.psum_scatter(grads[0], "col", scatter_dimension=0, tiled=True)
        item_total = lax.psum_scatter(grads[1], "row", scatter_dimension=0, tiled=True)
        parts = []

    own = [user_in[0], item_in[0]] if direct else [user_own, item_own]
    smooth = call(
        functools.partial(smooth_kernel, n_user, n_item),
        [struct(user_rows, rank, f32), struct(item_rows, rank, f32)],
        [pin(user_nbrs.T), item_adj] + user_in + item_in + own + [user_total],
        "smooth",
        spaces=[HBM] + [VMEM] * (3 + n_user + n_item) + [ANY],
        scratch=[
            pltpu.VMEM((block_users, rank), bf16),
            pltpu.VMEM((block_items, rank), bf16),
            pltpu.VMEM((knn, user_rows), jnp.int32),
            pltpu.VMEM((block_users, user_rows), bf16),
            pltpu.VMEM((words_of(knn, block_users), knn, user_rows), jnp.int32),
            pltpu.SemaphoreType.DMA,
        ],
        flops=COST_SMOOTH,
    )

    if direct:
        parts[1] = tie(parts[1], COST_IL, after=smooth[0])
    grad_users, grad_items = call(
        final_kernel,
        [struct(user_rows, rank, f32), struct(item_rows, rank, f32)],
        list(smooth) + [user_total, item_total] + parts,
        "finish",
        flops=8 * (user_rows + item_rows) * rank,
        nbytes=20 * (user_rows + item_rows) * rank,
    )
    return (grad_users, grad_items[None])


def solution(mesh):
    placed = (
        P(("row", "col"), None),
        P("col", "row", None),
        P("row", "col", None, None, None),
        P("row", "col", None),
        P("row", "col"),
        P("row", "col", None),
        P(("row", "col"), None),
        P("col", "row", None),
    )
    return jax.shard_map(
        functools.partial(local, mesh.shape["row"], mesh.shape["col"]),
        mesh=mesh,
        in_specs=placed,
        out_specs=(P(("row", "col"), None), P("col", "row", None)),
        check_vma=False,
    )
```

```python
import functools

import jax
import jax.numpy as jnp
from jax import lax
from jax.experimental import pallas as pl
from jax.experimental.pallas import tpu as pltpu
from jax.sharding import PartitionSpec as P

ALPHA = 0.5
DATA_SCALE = 0.0625
SMOOTH = 4.0
GROUP = 12
COST_NEAR = 10**10
COST_BE = 0
COST_COUNT = 0
COST_SMOOTH = 0
COST_IF = 0
COST_MARK = 10**8
COST_IN = 10**9
COST_IL = 10**10
VMEM = pl.BlockSpec(memory_space=pltpu.VMEM)
ANY = pl.BlockSpec(memory_space=pl.ANY)
HBM = pl.BlockSpec(memory_space=pltpu.HBM)


def call(kernel, outs, ins, name, spaces=None, scratch=(), flops=0, nbytes=0, limit=16):
    return pl.pallas_call(
        kernel,
        out_shape=outs,
        in_specs=spaces or [VMEM] * len(ins),
        out_specs=jax.tree.map(lambda _: VMEM, outs),
        scratch_shapes=scratch,
        cost_estimate=pl.CostEstimate(flops=flops, bytes_accessed=nbytes, transcendentals=0),
        compiler_params=pltpu.CompilerParams(vmem_limit_bytes=limit * 2**20),
        name=name,
    )(*ins)


def struct(rows, cols, dtype):
    return jax.ShapeDtypeStruct((rows, cols), dtype)


EXTRA = 16
OCTAVE = 64.0
TOP = 32400.0


def encode(block, out_ref, start):
    rows = block.shape[0]
    top = jnp.max(jnp.abs(block), axis=0, keepdims=True)
    level = jnp.ceil(jnp.log2(jnp.maximum(top, 1e-30)) * OCTAVE)
    fixed = jnp.round(block * (jnp.exp2(level * (-1.0 / OCTAVE)) * TOP))
    out_ref[start : start + rows, :] = fixed.astype(jnp.int32).astype(jnp.int16)
    spread = jnp.broadcast_to(level, (EXTRA, block.shape[1]))
    out_ref[start + rows : start + rows + EXTRA, :] = spread.astype(jnp.int32).astype(jnp.int16)


def decode(ref, start, rows):
    stop = start + rows
    level = ref[stop : stop + EXTRA, :].astype(jnp.int32).astype(jnp.float32)[:1]
    scale = jnp.exp2(level * (1.0 / OCTAVE)) * (1.0 / TOP)
    return ref[start:stop, :].astype(jnp.int32).astype(jnp.float32) * scale


def counts_of(nbrs, adj, digits):
    count, width = nbrs.shape
    blocks = adj.shape[0] // 128
    bits = count.bit_length()
    fields = 31 // bits
    words = -(-blocks // fields)
    step = 32
    index = nbrs[...]
    block = index >> 7
    digits[0] = index & 127
    for word in range(words):
        field = block - word * fields
        inside = (field >= 0) & (field < fields)
        digits[1 + word] = jnp.where(inside, 1 << (jnp.where(inside, field, 0) * bits), 0)
    for left in range(0, width, 128):
        lanes = slice(left, min(left + 128, width))
        span = lanes.stop - lanes.start

        def body(turn, _, lanes=lanes, span=span):
            here = turn * step + lax.broadcasted_iota(jnp.int32, (step, span), 0)
            totals = [jnp.zeros((step, span), jnp.int32)] * words
            for k in range(count):
                hit = jnp.broadcast_to(digits[0, k : k + 1, lanes], (step, span)) == here
                for word in range(words):
                    one = jnp.broadcast_to(digits[1 + word, k : k + 1, lanes], (step, span))
                    totals[word] = totals[word] + jnp.where(hit, one, 0)
            for block in range(blocks):
                word, field = divmod(block, fields)
                value = (totals[word] >> (field * bits)) & ((1 << bits) - 1)
                at = pl.ds(pl.multiple_of(block * 128 + turn * step, step), step)
                adj[at, lanes] = value.astype(jnp.float32).astype(jnp.bfloat16)
            return 0

        lax.fori_loop(0, 128 // step, body, 0)


def words_of(count, rows):
    return 1 + -(-(rows // 128) // (31 // count.bit_length()))


def count_kernel(nbrs, _, adj, near, digits, sem):
    copy = pltpu.make_async_copy(nbrs, near, sem)
    copy.start()
    copy.wait()
    counts_of(near, adj, digits)


def mark_kernel(source, out):
    out[...] = jnp.zeros_like(out)


def pair_kernel(own, other, *refs):
    out = refs[-1]
    rows = own.shape[0]
    out[:rows, :] = own[...]
    out[rows:, :] = other[...]


def tie_kernel(source, *refs):
    refs[-1][...] = source[...]


def tie(array, cost, after=None):
    if not cost:
        return array
    later = [] if after is None else [after]
    return call(
        tie_kernel,
        struct(*array.shape, array.dtype),
        [array] + later,
        "tie",
        spaces=[VMEM] + [ANY] * len(later),
        flops=cost,
    )


def col_masks():
    me = lax.axis_index("col")
    first = 2 + 2 * (me & 1)
    return me, first, 6 - first


def place(user_in, item_in, users, items):
    if len(user_in) == 1:
        users[...] = user_in[0][...]
        items[...] = item_in[0][...]
        return
    pair, second, swap_pair, swap_second = user_in
    me, first, other = col_masks()
    rows = pair.shape[0] // 2
    for ref, masks in (
        (pair, (0, first)),
        (second, (other, 6)),
        (swap_pair, (1, other ^ 1)),
        (swap_second, (first ^ 1, 7)),
    ):
        for k, mask in enumerate(masks):
            at = pl.ds(pl.multiple_of((me ^ mask) * rows, rows), rows)
            users[at, :] = ref[k * rows : (k + 1) * rows, :]
    me = lax.axis_index("row")
    rows = item_in[0].shape[0] // 2
    for ref, masks in zip(item_in, ((0, 2), (1, 3))):
        for k, mask in enumerate(masks):
            at = pl.ds(pl.multiple_of((me ^ mask) * rows, rows), rows)
            items[at, :] = ref[k * rows : (k + 1) * rows, :]


def main_kernel(n_user, n_item, direct, keep_in, sends_in, cells_in, ratings, *refs):
    user_in, refs = refs[:n_user], refs[n_user:]
    item_in, refs = refs[:n_item], refs[n_item:]
    outs, (keep, sends, cells, users, items, user_acc, item_acc, sem) = refs[:-8], refs[-8:]
    slots, tile = ratings.shape[:2]
    group = max(g for g in range(1, GROUP + 1) if slots % g == 0)
    item_count = items.shape[0] // tile
    copies = [
        pltpu.make_async_copy(src, dst, sem.at[k])
        for k, (src, dst) in enumerate(((keep_in, keep), (sends_in, sends), (cells_in, cells)))
    ]
    for copy in copies:
        copy.start()
    place(user_in, item_in, users, items)
    user_acc[...] = jnp.zeros_like(user_acc)
    item_acc[...] = jnp.zeros_like(item_acc)
    for copy in copies:
        copy.wait()
    live = keep[0, 0]
    for q in range(sends.shape[2]):
        live = live + sends[0, 0, q]

    def body(turn, _):
        work = []
        for g in range(group):
            slot = turn * group + g
            cell = cells[0, 0, slot]
            upper = cell // item_count
            lower = cell - upper * item_count
            user_at = pl.ds(pl.multiple_of(upper * tile, tile), tile)
            item_at = pl.ds(pl.multiple_of(lower * tile, tile), tile)
            left = users[user_at, :]
            right = items[item_at, :]
            product = lax.dot_general(
                left, right, (((1,), (1,)), ((), ())), preferred_element_type=jnp.float32
            )
            value = ratings[slot].astype(jnp.float32)
            error = (1.0 + ALPHA * value) * (product - jnp.where(value > 0, 1.0, 0.0))
            error = jnp.where(slot < live, error, 0.0).astype(jnp.bfloat16)
            work.append((user_at, item_at, left, right, error))
        for user_at, item_at, left, right, error in work:
            user_acc[user_at, :] += jnp.dot(error, right, preferred_element_type=jnp.float32)
            item_acc[item_at, :] += lax.dot_general(
                error, left, (((0,), (0,)), ((), ())), preferred_element_type=jnp.float32
            )
        return 0

    lax.fori_loop(0, (live + group - 1) // group, body, 0)

    if not direct:
        outs[0][...] = user_acc[...]
        outs[1][...] = item_acc[...]
        return
    user_keep, user_send, item_keep, item_near, item_relay = outs
    me, first, other = col_masks()
    rows = user_keep.shape[0] // 4
    for k, (mine, yours) in enumerate(((0, 1), (other, first ^ 1), (first, other ^ 1), (6, 7))):
        for out, mask in ((user_keep, mine), (user_send, yours)):
            at = pl.ds(pl.multiple_of((me ^ mask) * rows, rows), rows)
            out[k * rows : (k + 1) * rows, :] = user_acc[at, :]
    me = lax.axis_index("row")
    rows = item_keep.shape[0] // 2
    for k, (mine, yours, send) in enumerate(((0, 1, item_near), (2, 3, item_relay))):
        at = pl.ds(pl.multiple_of((me ^ mine) * rows, rows), rows)
        item_keep[k * rows : (k + 1) * rows, :] = item_acc[at, :]
        at = pl.ds(pl.multiple_of((me ^ yours) * rows, rows), rows)
        encode(item_acc[at, :], send, 0)


def chip_sum_kernel(keep, recv, total, send):
    rows = total.shape[0] // 2
    total[...] = keep[: 2 * rows, :] + recv[: 2 * rows, :]
    for k in range(2):
        at = slice((k + 2) * rows, (k + 3) * rows)
        encode(keep[at, :] + recv[at, :], send, k * (rows + EXTRA))


def fold_kernel(keep, recv, total, send):
    rows = total.shape[0]
    total[...] = keep[:rows, :] + decode(recv, 0, rows)
    encode(keep[rows:, :] + decode(recv, rows + EXTRA, rows), send, 0)


def relay_kernel(keep, recv, _, send):
    rows = keep.shape[0] // 2
    encode(keep[rows:, :] + decode(recv, 0, rows), send, 0)


def smooth_kernel(n_user, n_item, user_nbrs, item_adj, *refs):
    user_in, refs = refs[:n_user], refs[n_user:]
    item_in, refs = refs[:n_item], refs[n_item:]
    user_own, item_own, _, user_out, item_out, users, items, near, user_adj, digits, sem = refs
    copy = pltpu.make_async_copy(user_nbrs, near, sem)
    copy.start()
    place(user_in, item_in, users, items)
    copy.wait()
    counts_of(near, user_adj, digits)
    for adj, whole, own, out in (
        (user_adj, users, user_own, user_out),
        (item_adj, items, item_own, item_out),
    ):
        near = lax.dot_general(
            whole[...], adj[...], (((0,), (0,)), ((), ())), preferred_element_type=jnp.float32
        )
        mine = own[: out.shape[0], :].astype(jnp.float32)
        out[...] = SMOOTH * (mine - near.T * (1.0 / 16))


def final_kernel(user_smooth, item_smooth, user_total, item_total, *refs):
    user_out, item_out = refs[-2:]
    parts = refs[:-2]
    for smooth, total, recv, out in (
        (user_smooth, user_total, parts[:1], user_out),
        (item_smooth, item_total, parts[1:], item_out),
    ):
        rows = out.shape[0]
        whole = total[:rows, :]
        for part in recv:
            whole = whole + decode(part, 0, rows)
        out[...] = DATA_SCALE * whole + smooth[...]


def swap(array, axis, size, even, odd=None):
    odd = even if odd is None else odd
    return lax.ppermute(array, axis, [(i, i ^ (odd if i % 2 else even)) for i in range(size)])


def local(
    n_row, n_col,
    user_factors, item_factors, ratings, tile_cell, keep_count, send_count, user_nbrs, item_nbrs
):
    f32, bf16, i16 = jnp.float32, jnp.bfloat16, jnp.int16
    user_own, item_own = user_factors, item_factors[0]
    user_rows, rank = user_own.shape
    item_rows = item_own.shape[0]
    block_users, block_items = user_rows * n_col, item_rows * n_row
    pin = lambda array: pltpu.with_memory_space_constraint(array, pltpu.HBM)
    knn = user_nbrs.shape[1]
    slots, tile = ratings.shape[2:4]
    direct = n_col == 8 and n_row == 4

    if direct:
        far = swap(item_own, "row", n_row, 2)
        first = swap(user_own, "col", n_col, 2, 4)
        mark = call(
            mark_kernel, struct(8, 128, f32), [pin(ratings[0, 0])], "mark", spaces=[HBM],
            flops=COST_MARK,
        )
        user_pair = call(
            pair_kernel,
            struct(2 * user_rows, rank, bf16),
            [user_own, first, mark],
            "user_pair",
            spaces=[VMEM, VMEM, ANY],
        )
        second = tie(swap(user_pair, "col", n_col, 4, 2), COST_BE)
        item_pair = call(
            pair_kernel,
            struct(2 * item_rows, rank, bf16),
            [item_own, far],
            "item_pair",
        )
        near = swap(item_pair, "row", n_row, 1)
        near = tie(near, COST_NEAR)
        user_in = [user_pair, second, swap(user_pair, "col", n_col, 1), swap(second, "col", n_col, 1)]
        item_in = [item_pair, near]
    else:
        item_in = [lax.all_gather(item_own, "row", axis=0, tiled=True)]
        user_in = [lax.all_gather(user_own, "col", axis=0, tiled=True)]

    if direct:
        outs = [
            struct(block_users // 2, rank, f32),
            struct(block_users // 2, rank, f32),
            struct(block_items // 2, rank, f32),
            struct(item_rows + EXTRA, rank, i16),
            struct(item_rows + EXTRA, rank, i16),
        ]
    else:
        outs = [struct(block_users, rank, f32), struct(block_items, rank, f32)]
    n_user, n_item = len(user_in), len(item_in)
    grads = call(
        functools.partial(main_kernel, n_user, n_item, direct),
        outs,
        [keep_count, send_count, tile_cell, ratings[0, 0]] + user_in + item_in,
        "tiles",
        spaces=[HBM] * 3 + [VMEM] * (1 + n_user + n_item),
        scratch=[
            pltpu.SMEM(keep_count.shape, jnp.int32),
            pltpu.SMEM(send_count.shape, jnp.int32),
            pltpu.SMEM(tile_cell.shape, jnp.int32),
            pltpu.VMEM((block_users, rank), bf16),
            pltpu.VMEM((block_items, rank), bf16),
            pltpu.VMEM((block_users, rank), f32),
            pltpu.VMEM((block_items, rank), f32),
            pltpu.SemaphoreType.DMA((3,)),
        ],
        flops=6 * slots * tile * tile * rank,
        nbytes=ratings.size * 2,
        limit=24,
    )

    if direct:
        user_keep, user_send, item_keep, item_near, item_relay = grads
        user_recv = swap(user_send, "col", n_col, 1)
        item_relay = swap(item_relay, "row", n_row, 1)
        item_near = swap(item_near, "row", n_row, 1)
        pair_sum, chip_send = call(
            chip_sum_kernel,
            [struct(2 * user_rows, rank, f32), struct(2 * (user_rows + EXTRA), rank, i16)],
            [user_keep, user_recv],
            "chip_sum",
        )
        chip_recv = swap(chip_send, "col", n_col, 2, 4)
        item_adj = call(
            count_kernel,
            struct(block_items, item_rows, bf16),
            [pin(item_nbrs[0].T), pair_sum],
            "item_counts",
            spaces=[HBM, ANY],
            scratch=[
                pltpu.VMEM((knn, item_rows), jnp.int32),
                pltpu.VMEM((words_of(knn, block_items), knn, item_rows), jnp.int32),
                pltpu.SemaphoreType.DMA,
            ],
            flops=COST_COUNT,
        )
        item_last = call(
            relay_kernel,
            struct(item_rows + EXTRA, rank, i16),
            [item_keep, item_relay, item_adj],
            "item_relay",
            spaces=[VMEM, VMEM, ANY],
            flops=COST_IF,
        )
        item_last = swap(item_last, "row", n_row, 2)
        user_total, user_last = call(
            fold_kernel,
            [struct(user_rows, rank, f32), struct(user_rows + EXTRA, rank, i16)],
            [pair_sum, chip_recv],
            "user_fold",
            flops=4 * user_rows * rank,
            nbytes=16 * user_rows * rank,
        )
        parts = [swap(user_last, "col", n_col, 4, 2), item_last, item_near]
        item_total = item_keep
    else:
        user_total = lax.psum_scatter(grads[0], "col", scatter_dimension=0, tiled=True)
        item_total = lax.psum_scatter(grads[1], "row", scatter_dimension=0, tiled=True)
        parts = []
        item_adj = call(
            count_kernel,
            struct(block_items, item_rows, bf16),
            [pin(item_nbrs[0].T), user_total],
            "item_counts",
            spaces=[HBM, ANY],
            scratch=[
                pltpu.VMEM((knn, item_rows), jnp.int32),
                pltpu.VMEM((words_of(knn, block_items), knn, item_rows), jnp.int32),
                pltpu.SemaphoreType.DMA,
            ],
            flops=COST_COUNT,
        )

    own = [user_in[0], item_in[0]] if direct else [user_own, item_own]
    smooth = call(
        functools.partial(smooth_kernel, n_user, n_item),
        [struct(user_rows, rank, f32), struct(item_rows, rank, f32)],
        [pin(user_nbrs.T), item_adj] + user_in + item_in + own + [user_total],
        "smooth",
        spaces=[HBM] + [VMEM] * (3 + n_user + n_item) + [ANY],
        scratch=[
            pltpu.VMEM((block_users, rank), bf16),
            pltpu.VMEM((block_items, rank), bf16),
            pltpu.VMEM((knn, user_rows), jnp.int32),
            pltpu.VMEM((block_users, user_rows), bf16),
            pltpu.VMEM((words_of(knn, block_users), knn, user_rows), jnp.int32),
            pltpu.SemaphoreType.DMA,
        ],
        flops=COST_SMOOTH,
    )

    if direct:
        parts[1] = tie(parts[1], COST_IL, after=smooth[0])
        parts[2] = tie(parts[2], COST_IN)
    grad_users, grad_items = call(
        final_kernel,
        [struct(user_rows, rank, f32), struct(item_rows, rank, f32)],
        list(smooth) + [user_total, item_total] + parts,
        "finish",
        flops=8 * (user_rows + item_rows) * rank,
        nbytes=20 * (user_rows + item_rows) * rank,
    )
    return (grad_users, grad_items[None])


def solution(mesh):
    placed = (
        P(("row", "col"), None),
        P("col", "row", None),
        P("row", "col", None, None, None),
        P("row", "col", None),
        P("row", "col"),
        P("row", "col", None),
        P(("row", "col"), None),
        P("col", "row", None),
    )
    return jax.shard_map(
        functools.partial(local, mesh.shape["row"], mesh.shape["col"]),
        mesh=mesh,
        in_specs=placed,
        out_specs=(P(("row", "col"), None), P("col", "row", None)),
        check_vma=False,
    )
```

```python
import functools

import jax
import jax.numpy as jnp
from jax import lax
from jax.experimental import pallas as pl
from jax.experimental.pallas import tpu as pltpu
from jax.sharding import PartitionSpec as P

ALPHA = 0.5
DATA_SCALE = 0.0625
SMOOTH = 4.0
GROUP = 36
COST_NEAR = 10**10
COST_BE = 0
COST_PLAN = 0
COST_SMOOTH = 0
COST_IF = 0
COST_MARK = 10**8
COST_IN = 10**9
COST_IL = 10**10
VMEM = pl.BlockSpec(memory_space=pltpu.VMEM)
ANY = pl.BlockSpec(memory_space=pl.ANY)
HBM = pl.BlockSpec(memory_space=pltpu.HBM)
SMEM = pl.BlockSpec(memory_space=pltpu.SMEM)


def call(kernel, outs, ins, name, spaces=None, results=None, scratch=(), flops=0, nbytes=0, limit=16):
    return pl.pallas_call(
        kernel,
        out_shape=outs,
        in_specs=spaces or [VMEM] * len(ins),
        out_specs=results or jax.tree.map(lambda _: VMEM, outs),
        scratch_shapes=scratch,
        cost_estimate=pl.CostEstimate(flops=flops, bytes_accessed=nbytes, transcendentals=0),
        compiler_params=pltpu.CompilerParams(vmem_limit_bytes=limit * 2**20),
        name=name,
    )(*ins)


def struct(rows, cols, dtype):
    return jax.ShapeDtypeStruct((rows, cols), dtype)


EXTRA = 16
OCTAVE = 64.0
TOP = 32400.0


def encode(block, out_ref, start):
    rows = block.shape[0]
    top = jnp.max(jnp.abs(block), axis=0, keepdims=True)
    level = jnp.ceil(jnp.log2(jnp.maximum(top, 1e-30)) * OCTAVE)
    fixed = jnp.round(block * (jnp.exp2(level * (-1.0 / OCTAVE)) * TOP))
    out_ref[start : start + rows, :] = fixed.astype(jnp.int32).astype(jnp.int16)
    spread = jnp.broadcast_to(level, (EXTRA, block.shape[1]))
    out_ref[start + rows : start + rows + EXTRA, :] = spread.astype(jnp.int32).astype(jnp.int16)


def decode(ref, start, rows):
    stop = start + rows
    level = ref[stop : stop + EXTRA, :].astype(jnp.int32).astype(jnp.float32)[:1]
    scale = jnp.exp2(level * (1.0 / OCTAVE)) * (1.0 / TOP)
    return ref[start:stop, :].astype(jnp.int32).astype(jnp.float32) * scale


def counts_of(nbrs, adj, digits):
    count, width = nbrs.shape
    blocks = adj.shape[0] // 128
    bits = count.bit_length()
    fields = 31 // bits
    words = -(-blocks // fields)
    step = 32
    index = nbrs[...]
    block = index >> 7
    digits[0, :, :width] = index & 127
    for word in range(words):
        field = block - word * fields
        inside = (field >= 0) & (field < fields)
        digits[1 + word, :, :width] = jnp.where(inside, 1 << (jnp.where(inside, field, 0) * bits), 0)
    for left in range(0, width, 128):
        lanes = slice(left, min(left + 128, width))
        span = lanes.stop - lanes.start

        def body(turn, _, lanes=lanes, span=span):
            here = turn * step + lax.broadcasted_iota(jnp.int32, (step, span), 0)
            totals = [jnp.zeros((step, span), jnp.int32)] * words
            for k in range(count):
                hit = jnp.broadcast_to(digits[0, k : k + 1, lanes], (step, span)) == here
                for word in range(words):
                    one = jnp.broadcast_to(digits[1 + word, k : k + 1, lanes], (step, span))
                    totals[word] = totals[word] + jnp.where(hit, one, 0)
            for block in range(blocks):
                word, field = divmod(block, fields)
                value = (totals[word] >> (field * bits)) & ((1 << bits) - 1)
                at = pl.ds(pl.multiple_of(block * 128 + turn * step, step), step)
                adj[at, lanes] = value.astype(jnp.float32).astype(jnp.bfloat16)
            return 0

        lax.fori_loop(0, 128 // step, body, 0)


def words_of(count, rows):
    return 1 + -(-(rows // 128) // (31 // count.bit_length()))


def plan_kernel(keep, sends, cells, _, plan):
    live = keep[0, 0]
    for q in range(sends.shape[2]):
        live = live + sends[0, 0, q]
    plan[0] = live
    for slot in range(cells.shape[2]):
        plan[1 + slot] = cells[0, 0, slot]


def mark_kernel(source, out):
    out[...] = jnp.zeros_like(out)


def pair_kernel(own, other, *refs):
    out = refs[-1]
    rows = own.shape[0]
    out[:rows, :] = own[...]
    out[rows:, :] = other[...]


def tie_kernel(source, *refs):
    refs[-1][...] = source[...]


def tie(array, cost, after=None):
    if not cost:
        return array
    later = [] if after is None else [after]
    return call(
        tie_kernel,
        struct(*array.shape, array.dtype),
        [array] + later,
        "tie",
        spaces=[VMEM] + [ANY] * len(later),
        flops=cost,
    )


def col_masks():
    me = lax.axis_index("col")
    first = 2 + 2 * (me & 1)
    return me, first, 6 - first


def place(user_in, item_in, users, items):
    if len(user_in) == 1:
        users[...] = user_in[0][...]
        items[...] = item_in[0][...]
        return
    pair, second, swap_pair, swap_second = user_in
    me, first, other = col_masks()
    rows = pair.shape[0] // 2
    for ref, masks in (
        (pair, (0, first)),
        (second, (other, 6)),
        (swap_pair, (1, other ^ 1)),
        (swap_second, (first ^ 1, 7)),
    ):
        for k, mask in enumerate(masks):
            at = pl.ds(pl.multiple_of((me ^ mask) * rows, rows), rows)
            users[at, :] = ref[k * rows : (k + 1) * rows, :]
    me = lax.axis_index("row")
    rows = item_in[0].shape[0] // 2
    for ref, masks in zip(item_in, ((0, 2), (1, 3))):
        for k, mask in enumerate(masks):
            at = pl.ds(pl.multiple_of((me ^ mask) * rows, rows), rows)
            items[at, :] = ref[k * rows : (k + 1) * rows, :]


def main_kernel(n_user, n_item, direct, plan, ratings, *refs):
    user_in, refs = refs[:n_user], refs[n_user:]
    item_in, refs = refs[:n_item], refs[n_item:]
    outs, (users, items, user_acc, item_acc) = refs[:-4], refs[-4:]
    slots, tile = ratings.shape[:2]
    group = max(g for g in range(1, GROUP + 1) if slots % g == 0)
    item_count = items.shape[0] // tile
    place(user_in, item_in, users, items)
    user_acc[...] = jnp.zeros_like(user_acc)
    item_acc[...] = jnp.zeros_like(item_acc)
    live = plan[0]

    def body(turn, _):
        work = []
        for g in range(group):
            slot = turn * group + g
            cell = plan[1 + slot]
            upper = cell // item_count
            lower = cell - upper * item_count
            user_at = pl.ds(pl.multiple_of(upper * tile, tile), tile)
            item_at = pl.ds(pl.multiple_of(lower * tile, tile), tile)
            left = users[user_at, :]
            right = items[item_at, :]
            product = lax.dot_general(
                left, right, (((1,), (1,)), ((), ())), preferred_element_type=jnp.float32
            )
            value = ratings[slot].astype(jnp.float32)
            error = (1.0 + ALPHA * value) * (product - jnp.where(value > 0, 1.0, 0.0))
            error = jnp.where(slot < live, error, 0.0).astype(jnp.bfloat16)
            work.append((user_at, item_at, left, right, error))
        for user_at, item_at, left, right, error in work:
            user_acc[user_at, :] += jnp.dot(error, right, preferred_element_type=jnp.float32)
            item_acc[item_at, :] += lax.dot_general(
                error, left, (((0,), (0,)), ((), ())), preferred_element_type=jnp.float32
            )
        return 0

    lax.fori_loop(0, (live + group - 1) // group, body, 0)

    if not direct:
        outs[0][...] = user_acc[...]
        outs[1][...] = item_acc[...]
        return
    user_keep, user_send, item_keep, item_near, item_relay = outs
    me, first, other = col_masks()
    rows = user_keep.shape[0] // 4
    for k, (mine, yours) in enumerate(((0, 1), (other, first ^ 1), (first, other ^ 1), (6, 7))):
        for out, mask in ((user_keep, mine), (user_send, yours)):
            at = pl.ds(pl.multiple_of((me ^ mask) * rows, rows), rows)
            out[k * rows : (k + 1) * rows, :] = user_acc[at, :]
    me = lax.axis_index("row")
    rows = item_keep.shape[0] // 2
    for k, (mine, yours, send) in enumerate(((0, 1, item_near), (2, 3, item_relay))):
        at = pl.ds(pl.multiple_of((me ^ mine) * rows, rows), rows)
        item_keep[k * rows : (k + 1) * rows, :] = item_acc[at, :]
        at = pl.ds(pl.multiple_of((me ^ yours) * rows, rows), rows)
        encode(item_acc[at, :], send, 0)


def chip_sum_kernel(keep, recv, total, send):
    rows = total.shape[0] // 2
    total[...] = keep[: 2 * rows, :] + recv[: 2 * rows, :]
    for k in range(2):
        at = slice((k + 2) * rows, (k + 3) * rows)
        encode(keep[at, :] + recv[at, :], send, k * (rows + EXTRA))


def fold_kernel(keep, recv, total, send):
    rows = total.shape[0]
    total[...] = keep[:rows, :] + decode(recv, 0, rows)
    encode(keep[rows:, :] + decode(recv, rows + EXTRA, rows), send, 0)


def relay_kernel(keep, recv, send):
    rows = keep.shape[0] // 2
    encode(keep[rows:, :] + decode(recv, 0, rows), send, 0)


def smooth_kernel(n_user, n_item, user_nbrs, item_nbrs, *refs):
    user_in, refs = refs[:n_user], refs[n_user:]
    item_in, refs = refs[:n_item], refs[n_item:]
    user_own, item_own, _, user_out, item_out, users, items, *refs = refs
    user_near, item_near, user_adj, item_adj, digits, sem = refs
    copies = [
        pltpu.make_async_copy(user_nbrs, user_near, sem.at[0]),
        pltpu.make_async_copy(item_nbrs, item_near, sem.at[1]),
    ]
    for copy in copies:
        copy.start()
    place(user_in, item_in, users, items)
    copies[0].wait()
    counts_of(user_near, user_adj, digits)
    copies[1].wait()
    counts_of(item_near, item_adj, digits)
    for adj, whole, own, out in (
        (user_adj, users, user_own, user_out),
        (item_adj, items, item_own, item_out),
    ):
        near = lax.dot_general(
            whole[...], adj[...], (((0,), (0,)), ((), ())), preferred_element_type=jnp.float32
        )
        mine = own[: out.shape[0], :].astype(jnp.float32)
        out[...] = SMOOTH * (mine - near.T * (1.0 / 16))


def final_kernel(user_smooth, item_smooth, user_total, item_total, *refs):
    user_out, item_out = refs[-2:]
    parts = refs[:-2]
    for smooth, total, recv, out in (
        (user_smooth, user_total, parts[:1], user_out),
        (item_smooth, item_total, parts[1:], item_out),
    ):
        rows = out.shape[0]
        whole = total[:rows, :]
        for part in recv:
            whole = whole + decode(part, 0, rows)
        out[...] = DATA_SCALE * whole + smooth[...]


def swap(array, axis, size, even, odd=None):
    odd = even if odd is None else odd
    return lax.ppermute(array, axis, [(i, i ^ (odd if i % 2 else even)) for i in range(size)])


def local(
    n_row, n_col,
    user_factors, item_factors, ratings, tile_cell, keep_count, send_count, user_nbrs, item_nbrs
):
    f32, bf16, i16 = jnp.float32, jnp.bfloat16, jnp.int16
    user_own, item_own = user_factors, item_factors[0]
    user_rows, rank = user_own.shape
    item_rows = item_own.shape[0]
    block_users, block_items = user_rows * n_col, item_rows * n_row
    pin = lambda array: pltpu.with_memory_space_constraint(array, pltpu.HBM)
    knn = user_nbrs.shape[1]
    slots, tile = ratings.shape[2:4]
    direct = n_col == 8 and n_row == 4

    if direct:
        far = swap(item_own, "row", n_row, 2)
        first = swap(user_own, "col", n_col, 2, 4)
        mark = call(
            mark_kernel, struct(8, 128, f32), [pin(ratings[0, 0])], "mark", spaces=[HBM],
            flops=COST_MARK,
        )
        user_pair = call(
            pair_kernel,
            struct(2 * user_rows, rank, bf16),
            [user_own, first, mark],
            "user_pair",
            spaces=[VMEM, VMEM, ANY],
        )
        second = tie(swap(user_pair, "col", n_col, 4, 2), COST_BE)
        item_pair = call(
            pair_kernel,
            struct(2 * item_rows, rank, bf16),
            [item_own, far],
            "item_pair",
        )
        near = swap(item_pair, "row", n_row, 1)
        near = tie(near, COST_NEAR)
        user_in = [user_pair, second, swap(user_pair, "col", n_col, 1), swap(second, "col", n_col, 1)]
        item_in = [item_pair, near]
    else:
        item_in = [lax.all_gather(item_own, "row", axis=0, tiled=True)]
        user_in = [lax.all_gather(user_own, "col", axis=0, tiled=True)]

    if direct:
        outs = [
            struct(block_users // 2, rank, f32),
            struct(block_users // 2, rank, f32),
            struct(block_items // 2, rank, f32),
            struct(item_rows + EXTRA, rank, i16),
            struct(item_rows + EXTRA, rank, i16),
        ]
    else:
        outs = [struct(block_users, rank, f32), struct(block_items, rank, f32)]
    n_user, n_item = len(user_in), len(item_in)
    plan = call(
        plan_kernel,
        pltpu.SMEM((1 + slots,), jnp.int32),
        [keep_count, send_count, tile_cell, item_in[0]],
        "plan",
        spaces=[SMEM] * 3 + [ANY],
        results=SMEM,
        flops=COST_PLAN,
    )
    grads = call(
        functools.partial(main_kernel, n_user, n_item, direct),
        outs,
        [plan, ratings[0, 0]] + user_in + item_in,
        "tiles",
        spaces=[SMEM] + [VMEM] * (1 + n_user + n_item),
        scratch=[
            pltpu.VMEM((block_users, rank), bf16),
            pltpu.VMEM((block_items, rank), bf16),
            pltpu.VMEM((block_users, rank), f32),
            pltpu.VMEM((block_items, rank), f32),
        ],
        flops=6 * slots * tile * tile * rank,
        nbytes=ratings.size * 2,
        limit=24,
    )

    if direct:
        user_keep, user_send, item_keep, item_near, item_relay = grads
        user_recv = swap(user_send, "col", n_col, 1)
        item_relay = swap(item_relay, "row", n_row, 1)
        item_near = swap(item_near, "row", n_row, 1)
        pair_sum, chip_send = call(
            chip_sum_kernel,
            [struct(2 * user_rows, rank, f32), struct(2 * (user_rows + EXTRA), rank, i16)],
            [user_keep, user_recv],
            "chip_sum",
        )
        chip_recv = swap(chip_send, "col", n_col, 2, 4)
        item_last = call(
            relay_kernel,
            struct(item_rows + EXTRA, rank, i16),
            [item_keep, item_relay],
            "item_relay",
            flops=COST_IF,
        )
        item_last = swap(item_last, "row", n_row, 2)
        user_total, user_last = call(
            fold_kernel,
            [struct(user_rows, rank, f32), struct(user_rows + EXTRA, rank, i16)],
            [pair_sum, chip_recv],
            "user_fold",
            flops=4 * user_rows * rank,
            nbytes=16 * user_rows * rank,
        )
        parts = [swap(user_last, "col", n_col, 4, 2), item_last, item_near]
        item_total = item_keep
    else:
        user_total = lax.psum_scatter(grads[0], "col", scatter_dimension=0, tiled=True)
        item_total = lax.psum_scatter(grads[1], "row", scatter_dimension=0, tiled=True)
        parts = []

    digit_rows = words_of(knn, max(block_users, block_items))
    own = [user_in[0], item_in[0]] if direct else [user_own, item_own]
    smooth = call(
        functools.partial(smooth_kernel, n_user, n_item),
        [struct(user_rows, rank, f32), struct(item_rows, rank, f32)],
        [pin(user_nbrs.T), pin(item_nbrs[0].T)] + user_in + item_in + own + [user_total],
        "smooth",
        spaces=[HBM] * 2 + [VMEM] * (2 + n_user + n_item) + [ANY],
        scratch=[
            pltpu.VMEM((block_users, rank), bf16),
            pltpu.VMEM((block_items, rank), bf16),
            pltpu.VMEM((knn, user_rows), jnp.int32),
            pltpu.VMEM((knn, item_rows), jnp.int32),
            pltpu.VMEM((block_users, user_rows), bf16),
            pltpu.VMEM((block_items, item_rows), bf16),
            pltpu.VMEM((digit_rows, knn, max(user_rows, item_rows)), jnp.int32),
            pltpu.SemaphoreType.DMA((2,)),
        ],
        flops=COST_SMOOTH,
    )

    if direct:
        parts[1] = tie(parts[1], COST_IL, after=smooth[0])
        parts[2] = tie(parts[2], COST_IN)
    grad_users, grad_items = call(
        final_kernel,
        [struct(user_rows, rank, f32), struct(item_rows, rank, f32)],
        list(smooth) + [user_total, item_total] + parts,
        "finish",
        flops=8 * (user_rows + item_rows) * rank,
        nbytes=20 * (user_rows + item_rows) * rank,
    )
    return (grad_users, grad_items[None])


def solution(mesh):
    placed = (
        P(("row", "col"), None),
        P("col", "row", None),
        P("row", "col", None, None, None),
        P("row", "col", None),
        P("row", "col"),
        P("row", "col", None),
        P(("row", "col"), None),
        P("col", "row", None),
    )
    return jax.shard_map(
        functools.partial(local, mesh.shape["row"], mesh.shape["col"]),
        mesh=mesh,
        in_specs=placed,
        out_specs=(P(("row", "col"), None), P("col", "row", None)),
        check_vma=False,
    )
```

```python
import functools

import jax
import jax.numpy as jnp
from jax import lax
from jax.experimental import pallas as pl
from jax.experimental.pallas import tpu as pltpu
from jax.sharding import PartitionSpec as P

ALPHA = 0.5
DATA_SCALE = 0.0625
SMOOTH = 4.0
GROUP = 36
COST_NEAR = 10**10
COST_LEVEL = 6*10**8
COST_CROSS = 0
COST_PLAN = 0
COST_SMOOTH = 0
COST_IF = 0
COST_MARK = 10**8
COST_RL = 6*10**8
COST_FW = 0
COST_IL = 10**10
VMEM = pl.BlockSpec(memory_space=pltpu.VMEM)
ANY = pl.BlockSpec(memory_space=pl.ANY)
HBM = pl.BlockSpec(memory_space=pltpu.HBM)
SMEM = pl.BlockSpec(memory_space=pltpu.SMEM)


def call(kernel, outs, ins, name, spaces=None, results=None, scratch=(), flops=0, nbytes=0, limit=16):
    return pl.pallas_call(
        kernel,
        out_shape=outs,
        in_specs=spaces or [VMEM] * len(ins),
        out_specs=results or jax.tree.map(lambda _: VMEM, outs),
        scratch_shapes=scratch,
        cost_estimate=pl.CostEstimate(flops=flops, bytes_accessed=nbytes, transcendentals=0),
        compiler_params=pltpu.CompilerParams(vmem_limit_bytes=limit * 2**20),
        name=name,
    )(*ins)


def struct(rows, cols, dtype):
    return jax.ShapeDtypeStruct((rows, cols), dtype)


EXTRA = 16
OCTAVE = 64.0
TOP = 32400.0


def encode(block, out_ref, start):
    rows = block.shape[0]
    top = jnp.max(jnp.abs(block), axis=0, keepdims=True)
    level = jnp.ceil(jnp.log2(jnp.maximum(top, 1e-30)) * OCTAVE)
    fixed = jnp.round(block * (jnp.exp2(level * (-1.0 / OCTAVE)) * TOP))
    out_ref[start : start + rows, :] = fixed.astype(jnp.int32).astype(jnp.int16)
    spread = jnp.broadcast_to(level, (EXTRA, block.shape[1]))
    out_ref[start + rows : start + rows + EXTRA, :] = spread.astype(jnp.int32).astype(jnp.int16)


def decode(ref, start, rows):
    stop = start + rows
    level = ref[stop : stop + EXTRA, :].astype(jnp.int32).astype(jnp.float32)[:1]
    scale = jnp.exp2(level * (1.0 / OCTAVE)) * (1.0 / TOP)
    return ref[start:stop, :].astype(jnp.int32).astype(jnp.float32) * scale


def counts_of(nbrs, adj, digits):
    count, width = nbrs.shape
    blocks = adj.shape[0] // 128
    bits = count.bit_length()
    fields = 31 // bits
    words = -(-blocks // fields)
    step = 32
    index = nbrs[...]
    block = index >> 7
    digits[0, :, :width] = index & 127
    for word in range(words):
        field = block - word * fields
        inside = (field >= 0) & (field < fields)
        digits[1 + word, :, :width] = jnp.where(inside, 1 << (jnp.where(inside, field, 0) * bits), 0)
    for left in range(0, width, 128):
        lanes = slice(left, min(left + 128, width))
        span = lanes.stop - lanes.start

        def body(turn, _, lanes=lanes, span=span):
            here = turn * step + lax.broadcasted_iota(jnp.int32, (step, span), 0)
            totals = [jnp.zeros((step, span), jnp.int32)] * words
            for k in range(count):
                hit = jnp.broadcast_to(digits[0, k : k + 1, lanes], (step, span)) == here
                for word in range(words):
                    one = jnp.broadcast_to(digits[1 + word, k : k + 1, lanes], (step, span))
                    totals[word] = totals[word] + jnp.where(hit, one, 0)
            for block in range(blocks):
                word, field = divmod(block, fields)
                value = (totals[word] >> (field * bits)) & ((1 << bits) - 1)
                at = pl.ds(pl.multiple_of(block * 128 + turn * step, step), step)
                adj[at, lanes] = value.astype(jnp.float32).astype(jnp.bfloat16)
            return 0

        lax.fori_loop(0, 128 // step, body, 0)


def words_of(count, rows):
    return 1 + -(-(rows // 128) // (31 // count.bit_length()))


def plan_kernel(keep, sends, cells, _, plan):
    live = keep[0, 0]
    for q in range(sends.shape[2]):
        live = live + sends[0, 0, q]
    plan[0] = live
    for slot in range(cells.shape[2]):
        plan[1 + slot] = cells[0, 0, slot]


def mark_kernel(source, out):
    out[...] = jnp.zeros_like(out)


def user_pair_kernel(own, other, _, out, held):
    pair_kernel(own, other, out)
    held[...] = own[...]


def pair_kernel(own, other, out):
    rows = own.shape[0]
    out[:rows, :] = own[...]
    out[rows:, :] = other[...]


def tie_kernel(source, *refs):
    refs[-1][...] = source[...]


def tie(array, cost, after=None):
    if not cost:
        return array
    later = [] if after is None else [after]
    return call(
        tie_kernel,
        struct(*array.shape, array.dtype),
        [array] + later,
        "tie",
        spaces=[VMEM] + [ANY] * len(later),
        flops=cost,
    )


def col_masks():
    me = lax.axis_index("col")
    cross = 2 + 4 * (me & 1)
    return me, cross, 8 - cross


def place(user_in, item_in, users, items):
    if len(user_in) == 1:
        users[...] = user_in[0][...]
        items[...] = item_in[0][...]
        return
    pair, level, swap_level, cross, swap_cross = user_in
    me, mine, yours = col_masks()
    rows = level.shape[0]
    for ref, masks in (
        (pair, (0, 1)),
        (level, (4,)),
        (swap_level, (5,)),
        (cross, (mine, mine ^ 1)),
        (swap_cross, (yours ^ 1, yours)),
    ):
        for k, mask in enumerate(masks):
            at = pl.ds(pl.multiple_of((me ^ mask) * rows, rows), rows)
            users[at, :] = ref[k * rows : (k + 1) * rows, :]
    me = lax.axis_index("row")
    rows = item_in[0].shape[0] // 2
    for ref, masks in zip(item_in, ((0, 2), (1, 3))):
        for k, mask in enumerate(masks):
            at = pl.ds(pl.multiple_of((me ^ mask) * rows, rows), rows)
            items[at, :] = ref[k * rows : (k + 1) * rows, :]


def main_kernel(n_user, n_item, direct, plan, ratings, *refs):
    user_in, refs = refs[:n_user], refs[n_user:]
    item_in, refs = refs[:n_item], refs[n_item:]
    outs, (users, items, user_acc, item_acc) = refs[:-4], refs[-4:]
    slots, tile = ratings.shape[:2]
    group = max(g for g in range(1, GROUP + 1) if slots % g == 0)
    item_count = items.shape[0] // tile
    place(user_in, item_in, users, items)
    user_acc[...] = jnp.zeros_like(user_acc)
    item_acc[...] = jnp.zeros_like(item_acc)
    live = plan[0]

    def body(turn, _):
        work = []
        for g in range(group):
            slot = turn * group + g
            cell = plan[1 + slot]
            upper = cell // item_count
            lower = cell - upper * item_count
            user_at = pl.ds(pl.multiple_of(upper * tile, tile), tile)
            item_at = pl.ds(pl.multiple_of(lower * tile, tile), tile)
            left = users[user_at, :]
            right = items[item_at, :]
            product = lax.dot_general(
                left, right, (((1,), (1,)), ((), ())), preferred_element_type=jnp.float32
            )
            value = ratings[slot].astype(jnp.float32)
            error = (1.0 + ALPHA * value) * (product - jnp.where(value > 0, 1.0, 0.0))
            error = jnp.where(slot < live, error, 0.0).astype(jnp.bfloat16)
            work.append((user_at, item_at, left, right, error))
        for user_at, item_at, left, right, error in work:
            user_acc[user_at, :] += jnp.dot(error, right, preferred_element_type=jnp.float32)
            item_acc[item_at, :] += lax.dot_general(
                error, left, (((0,), (0,)), ((), ())), preferred_element_type=jnp.float32
            )
        return 0

    lax.fori_loop(0, (live + group - 1) // group, body, 0)

    if not direct:
        outs[0][...] = user_acc[...]
        outs[1][...] = item_acc[...]
        return
    user_keep, user_send, item_keep, item_send = outs
    me, mine, yours = col_masks()
    rows = user_keep.shape[0] // 4
    for out, masks in (
        (user_keep, (0, 4, mine, mine ^ 1)),
        (user_send, (1, 5, yours ^ 1, yours)),
    ):
        for k, mask in enumerate(masks):
            at = pl.ds(pl.multiple_of((me ^ mask) * rows, rows), rows)
            out[k * rows : (k + 1) * rows, :] = user_acc[at, :]
    me = lax.axis_index("row")
    rows = item_keep.shape[0] // 2
    for k, (own, other) in enumerate(((0, 1), (2, 3))):
        at = pl.ds(pl.multiple_of((me ^ own) * rows, rows), rows)
        item_keep[k * rows : (k + 1) * rows, :] = item_acc[at, :]
        at = pl.ds(pl.multiple_of((me ^ other) * rows, rows), rows)
        encode(item_acc[at, :], item_send, k * (rows + EXTRA))


def chip_sum_kernel(keep, recv, total, level, cross):
    rows = total.shape[0]
    total[...] = keep[:rows, :] + recv[:rows, :]
    for k, (send, start) in enumerate(((level, 0), (cross, 0), (cross, rows + EXTRA)), 1):
        at = slice(k * rows, (k + 1) * rows)
        encode(keep[at, :] + recv[at, :], send, start)


def forward_kernel(recv, send):
    send[...] = recv[send.shape[0] :, :]


def relay_kernel(keep, recv, send):
    rows = keep.shape[0] // 2
    encode(keep[rows:, :] + decode(recv, rows + EXTRA, rows), send, 0)


def smooth_kernel(n_user, n_item, user_nbrs, item_nbrs, *refs):
    user_in, refs = refs[:n_user], refs[n_user:]
    item_in, refs = refs[:n_item], refs[n_item:]
    user_own, item_own, _, user_out, item_out, users, items, *refs = refs
    user_adj, item_adj, digits = refs
    place(user_in, item_in, users, items)
    counts_of(user_nbrs, user_adj, digits)
    counts_of(item_nbrs, item_adj, digits)
    for adj, whole, own, out in (
        (user_adj, users, user_own, user_out),
        (item_adj, items, item_own, item_out),
    ):
        near = lax.dot_general(
            whole[...], adj[...], (((0,), (0,)), ((), ())), preferred_element_type=jnp.float32
        )
        mine = own[: out.shape[0], :].astype(jnp.float32)
        out[...] = SMOOTH * (mine - near.T * (1.0 / 16))


def final_kernel(n_user, user_smooth, item_smooth, user_total, item_total, *refs):
    user_out, item_out = refs[-2:]
    parts = refs[:-2]
    for smooth, total, recv, out in (
        (user_smooth, user_total, parts[:n_user], user_out),
        (item_smooth, item_total, parts[n_user:], item_out),
    ):
        rows = out.shape[0]
        whole = total[:rows, :]
        for part in recv:
            whole = whole + decode(part, 0, rows)
        out[...] = DATA_SCALE * whole + smooth[...]


def swap(array, axis, size, even, odd=None):
    odd = even if odd is None else odd
    return lax.ppermute(array, axis, [(i, i ^ (odd if i % 2 else even)) for i in range(size)])


def local(
    n_row, n_col,
    user_factors, item_factors, ratings, tile_cell, keep_count, send_count, user_nbrs, item_nbrs
):
    f32, bf16, i16 = jnp.float32, jnp.bfloat16, jnp.int16
    user_own, item_own = user_factors, item_factors[0]
    user_rows, rank = user_own.shape
    item_rows = item_own.shape[0]
    block_users, block_items = user_rows * n_col, item_rows * n_row
    pin = lambda array: pltpu.with_memory_space_constraint(array, pltpu.HBM)
    knn = user_nbrs.shape[1]
    slots, tile = ratings.shape[2:4]
    direct = n_col == 8 and n_row == 4

    if direct:
        far = swap(item_own, "row", n_row, 2)
        other = swap(user_own, "col", n_col, 1)
        mark = call(
            mark_kernel, struct(8, 128, f32), [pin(ratings[0, 0])], "mark", spaces=[HBM],
            flops=COST_MARK,
        )
        user_pair, user_held = call(
            user_pair_kernel,
            [struct(2 * user_rows, rank, bf16), struct(user_rows, rank, bf16)],
            [user_own, other, mark],
            "user_pair",
            spaces=[VMEM, VMEM, ANY],
        )
        cross = tie(swap(user_pair, "col", n_col, 2, 6), COST_CROSS)
        level = tie(swap(user_held, "col", n_col, 4), COST_LEVEL)
        item_pair = call(
            pair_kernel,
            struct(2 * item_rows, rank, bf16),
            [item_own, far],
            "item_pair",
        )
        near = swap(item_pair, "row", n_row, 1)
        near = tie(near, COST_NEAR)
        user_in = [
            user_pair, level, swap(level, "col", n_col, 1), cross, swap(cross, "col", n_col, 1),
        ]
        item_in = [item_pair, near]
    else:
        item_in = [lax.all_gather(item_own, "row", axis=0, tiled=True)]
        user_in = [lax.all_gather(user_own, "col", axis=0, tiled=True)]

    if direct:
        outs = [
            struct(block_users // 2, rank, f32),
            struct(block_users // 2, rank, f32),
            struct(block_items // 2, rank, f32),
            struct(2 * (item_rows + EXTRA), rank, i16),
        ]
    else:
        outs = [struct(block_users, rank, f32), struct(block_items, rank, f32)]
    n_user, n_item = len(user_in), len(item_in)
    plan = call(
        plan_kernel,
        pltpu.SMEM((1 + slots,), jnp.int32),
        [keep_count, send_count, tile_cell, item_in[0]],
        "plan",
        spaces=[SMEM] * 3 + [ANY],
        results=SMEM,
        flops=COST_PLAN,
    )
    grads = call(
        functools.partial(main_kernel, n_user, n_item, direct),
        outs,
        [plan, ratings[0, 0]] + user_in + item_in,
        "tiles",
        spaces=[SMEM] + [VMEM] * (1 + n_user + n_item),
        scratch=[
            pltpu.VMEM((block_users, rank), bf16),
            pltpu.VMEM((block_items, rank), bf16),
            pltpu.VMEM((block_users, rank), f32),
            pltpu.VMEM((block_items, rank), f32),
        ],
        flops=6 * slots * tile * tile * rank,
        nbytes=ratings.size * 2,
        limit=24,
    )

    if direct:
        user_keep, user_send, item_keep, item_send = grads
        user_recv = swap(user_send, "col", n_col, 1)
        item_recv = swap(item_send, "row", n_row, 1)
        item_last = call(
            relay_kernel,
            struct(item_rows + EXTRA, rank, i16),
            [item_keep, item_recv],
            "item_relay",
            flops=COST_IF,
        )
        item_last = swap(item_last, "row", n_row, 2)
        user_total, level, cross = call(
            chip_sum_kernel,
            [
                struct(user_rows, rank, f32),
                struct(user_rows + EXTRA, rank, i16),
                struct(2 * (user_rows + EXTRA), rank, i16),
            ],
            [user_keep, user_recv],
            "chip_sum",
        )
        cross = swap(cross, "col", n_col, 2, 6)
        level = tie(swap(level, "col", n_col, 4), COST_RL)
        behind = call(
            forward_kernel, struct(user_rows + EXTRA, rank, i16), [cross], "forward",
            flops=COST_FW,
        )
        user_parts = [level, cross, swap(behind, "col", n_col, 1)]
        item_parts = [item_recv, item_last]
        item_total = item_keep
    else:
        user_total = lax.psum_scatter(grads[0], "col", scatter_dimension=0, tiled=True)
        item_total = lax.psum_scatter(grads[1], "row", scatter_dimension=0, tiled=True)
        user_parts, item_parts = [], []
        behind = user_total

    digit_rows = words_of(knn, max(block_users, block_items))
    own = [user_in[0], item_in[0]] if direct else [user_own, item_own]
    smooth = call(
        functools.partial(smooth_kernel, n_user, n_item),
        [struct(user_rows, rank, f32), struct(item_rows, rank, f32)],
        [user_nbrs.T, item_nbrs[0].T] + user_in + item_in + own + [behind],
        "smooth",
        spaces=[VMEM] * (4 + n_user + n_item) + [ANY],
        scratch=[
            pltpu.VMEM((block_users, rank), bf16),
            pltpu.VMEM((block_items, rank), bf16),
            pltpu.VMEM((block_users, user_rows), bf16),
            pltpu.VMEM((block_items, item_rows), bf16),
            pltpu.VMEM((digit_rows, knn, max(user_rows, item_rows)), jnp.int32),
        ],
        flops=COST_SMOOTH,
    )

    if direct:
        item_parts[1] = tie(item_parts[1], COST_IL, after=smooth[0])
    grad_users, grad_items = call(
        functools.partial(final_kernel, len(user_parts)),
        [struct(user_rows, rank, f32), struct(item_rows, rank, f32)],
        list(smooth) + [user_total, item_total] + user_parts + item_parts,
        "finish",
        flops=8 * (user_rows + item_rows) * rank,
        nbytes=20 * (user_rows + item_rows) * rank,
    )
    return (grad_users, grad_items[None])


def solution(mesh):
    placed = (
        P(("row", "col"), None),
        P("col", "row", None),
        P("row", "col", None, None, None),
        P("row", "col", None),
        P("row", "col"),
        P("row", "col", None),
        P(("row", "col"), None),
        P("col", "row", None),
    )
    return jax.shard_map(
        functools.partial(local, mesh.shape["row"], mesh.shape["col"]),
        mesh=mesh,
        in_specs=placed,
        out_specs=(P(("row", "col"), None), P("col", "row", None)),
        check_vma=False,
    )
```

```python
import functools

import jax
import jax.numpy as jnp
from jax import lax
from jax.experimental import pallas as pl
from jax.experimental.pallas import tpu as pltpu
from jax.sharding import PartitionSpec as P

ALPHA = 0.5
DATA_SCALE = 0.0625
SMOOTH = 4.0
GROUP = 36
COST_NEAR = 10**10
COST_LEVEL = 6*10**8
COST_CROSS = 0
COST_PLAN = 0
COST_SMOOTH = 0
COST_IF = 0
COST_MARK = 10**8
COST_UC = 0
COST_RL = 6*10**8
COST_FW = 0
COST_IL = 10**10
VMEM = pl.BlockSpec(memory_space=pltpu.VMEM)
ANY = pl.BlockSpec(memory_space=pl.ANY)
HBM = pl.BlockSpec(memory_space=pltpu.HBM)
SMEM = pl.BlockSpec(memory_space=pltpu.SMEM)


def call(kernel, outs, ins, name, spaces=None, results=None, scratch=(), flops=0, nbytes=0, limit=16):
    return pl.pallas_call(
        kernel,
        out_shape=outs,
        in_specs=spaces or [VMEM] * len(ins),
        out_specs=results or jax.tree.map(lambda _: VMEM, outs),
        scratch_shapes=scratch,
        cost_estimate=pl.CostEstimate(flops=flops, bytes_accessed=nbytes, transcendentals=0),
        compiler_params=pltpu.CompilerParams(vmem_limit_bytes=limit * 2**20),
        name=name,
    )(*ins)


def struct(rows, cols, dtype):
    return jax.ShapeDtypeStruct((rows, cols), dtype)


EXTRA = 16
OCTAVE = 64.0
TOP = 32400.0


def encode(block, out_ref, start):
    rows = block.shape[0]
    top = jnp.max(jnp.abs(block), axis=0, keepdims=True)
    level = jnp.ceil(jnp.log2(jnp.maximum(top, 1e-30)) * OCTAVE)
    fixed = jnp.round(block * (jnp.exp2(level * (-1.0 / OCTAVE)) * TOP))
    out_ref[start : start + rows, :] = fixed.astype(jnp.int32).astype(jnp.int16)
    spread = jnp.broadcast_to(level, (EXTRA, block.shape[1]))
    out_ref[start + rows : start + rows + EXTRA, :] = spread.astype(jnp.int32).astype(jnp.int16)


def decode(ref, start, rows):
    stop = start + rows
    level = ref[stop : stop + EXTRA, :].astype(jnp.int32).astype(jnp.float32)[:1]
    scale = jnp.exp2(level * (1.0 / OCTAVE)) * (1.0 / TOP)
    return ref[start:stop, :].astype(jnp.int32).astype(jnp.float32) * scale


def counts_of(nbrs, adj, digits):
    count, width = nbrs.shape
    blocks = adj.shape[0] // 128
    bits = count.bit_length()
    fields = 31 // bits
    words = -(-blocks // fields)
    step = 32
    index = nbrs[...]
    block = index >> 7
    digits[0] = index & 127
    for word in range(words):
        field = block - word * fields
        inside = (field >= 0) & (field < fields)
        digits[1 + word] = jnp.where(inside, 1 << (jnp.where(inside, field, 0) * bits), 0)
    for left in range(0, width, 128):
        lanes = slice(left, min(left + 128, width))
        span = lanes.stop - lanes.start

        def body(turn, _, lanes=lanes, span=span):
            here = turn * step + lax.broadcasted_iota(jnp.int32, (step, span), 0)
            totals = [jnp.zeros((step, span), jnp.int32)] * words
            for k in range(count):
                hit = jnp.broadcast_to(digits[0, k : k + 1, lanes], (step, span)) == here
                for word in range(words):
                    one = jnp.broadcast_to(digits[1 + word, k : k + 1, lanes], (step, span))
                    totals[word] = totals[word] + jnp.where(hit, one, 0)
            for block in range(blocks):
                word, field = divmod(block, fields)
                value = (totals[word] >> (field * bits)) & ((1 << bits) - 1)
                at = pl.ds(pl.multiple_of(block * 128 + turn * step, step), step)
                adj[at, lanes] = value.astype(jnp.float32).astype(jnp.bfloat16)
            return 0

        lax.fori_loop(0, 128 // step, body, 0)


def words_of(count, rows):
    return 1 + -(-(rows // 128) // (31 // count.bit_length()))


def plan_kernel(keep, sends, cells, _, plan):
    live = keep[0, 0]
    for q in range(sends.shape[2]):
        live = live + sends[0, 0, q]
    plan[0] = live
    for slot in range(cells.shape[2]):
        plan[1 + slot] = cells[0, 0, slot]


def mark_kernel(source, out):
    out[...] = jnp.zeros_like(out)


def user_pair_kernel(own, other, _, out, held):
    pair_kernel(own, other, out)
    held[...] = own[...]


def pair_kernel(own, other, out):
    rows = own.shape[0]
    out[:rows, :] = own[...]
    out[rows:, :] = other[...]


def tie_kernel(source, *refs):
    refs[-1][...] = source[...]


def tie(array, cost, after=None):
    if not cost:
        return array
    later = [] if after is None else [after]
    return call(
        tie_kernel,
        struct(*array.shape, array.dtype),
        [array] + later,
        "tie",
        spaces=[VMEM] + [ANY] * len(later),
        flops=cost,
    )


def col_masks():
    me = lax.axis_index("col")
    cross = 2 + 4 * (me & 1)
    return me, cross, 8 - cross


def place(user_in, item_in, users, items):
    if len(user_in) == 1:
        users[...] = user_in[0][...]
        items[...] = item_in[0][...]
        return
    pair, level, swap_level, cross, swap_cross = user_in
    me, mine, yours = col_masks()
    rows = level.shape[0]
    for ref, masks in (
        (pair, (0, 1)),
        (level, (4,)),
        (swap_level, (5,)),
        (cross, (mine, mine ^ 1)),
        (swap_cross, (yours ^ 1, yours)),
    ):
        for k, mask in enumerate(masks):
            at = pl.ds(pl.multiple_of((me ^ mask) * rows, rows), rows)
            users[at, :] = ref[k * rows : (k + 1) * rows, :]
    me = lax.axis_index("row")
    rows = item_in[0].shape[0] // 2
    for ref, masks in zip(item_in, ((0, 2), (1, 3))):
        for k, mask in enumerate(masks):
            at = pl.ds(pl.multiple_of((me ^ mask) * rows, rows), rows)
            items[at, :] = ref[k * rows : (k + 1) * rows, :]


def main_kernel(n_user, n_item, direct, plan, ratings, *refs):
    user_in, refs = refs[:n_user], refs[n_user:]
    item_in, refs = refs[:n_item], refs[n_item:]
    outs, (users, items, user_acc, item_acc) = refs[:-4], refs[-4:]
    slots, tile = ratings.shape[:2]
    group = max(g for g in range(1, GROUP + 1) if slots % g == 0)
    item_count = items.shape[0] // tile
    place(user_in, item_in, users, items)
    user_acc[...] = jnp.zeros_like(user_acc)
    item_acc[...] = jnp.zeros_like(item_acc)
    live = plan[0]

    def body(turn, _):
        work = []
        for g in range(group):
            slot = turn * group + g
            cell = plan[1 + slot]
            upper = cell // item_count
            lower = cell - upper * item_count
            user_at = pl.ds(pl.multiple_of(upper * tile, tile), tile)
            item_at = pl.ds(pl.multiple_of(lower * tile, tile), tile)
            left = users[user_at, :]
            right = items[item_at, :]
            product = lax.dot_general(
                left, right, (((1,), (1,)), ((), ())), preferred_element_type=jnp.float32
            )
            value = ratings[slot].astype(jnp.float32)
            error = (1.0 + ALPHA * value) * (product - jnp.where(value > 0, 1.0, 0.0))
            error = jnp.where(slot < live, error, 0.0).astype(jnp.bfloat16)
            work.append((user_at, item_at, left, right, error))
        for user_at, item_at, left, right, error in work:
            user_acc[user_at, :] += jnp.dot(error, right, preferred_element_type=jnp.float32)
            item_acc[item_at, :] += lax.dot_general(
                error, left, (((0,), (0,)), ((), ())), preferred_element_type=jnp.float32
            )
        return 0

    lax.fori_loop(0, (live + group - 1) // group, body, 0)

    if not direct:
        outs[0][...] = user_acc[...]
        outs[1][...] = item_acc[...]
        return
    user_keep, user_send, item_keep, item_send = outs
    me, mine, yours = col_masks()
    rows = user_keep.shape[0] // 4
    for out, masks in (
        (user_keep, (0, 4, mine, mine ^ 1)),
        (user_send, (1, 5, yours ^ 1, yours)),
    ):
        for k, mask in enumerate(masks):
            at = pl.ds(pl.multiple_of((me ^ mask) * rows, rows), rows)
            out[k * rows : (k + 1) * rows, :] = user_acc[at, :]
    me = lax.axis_index("row")
    rows = item_keep.shape[0] // 2
    for k, (own, other) in enumerate(((0, 1), (2, 3))):
        at = pl.ds(pl.multiple_of((me ^ own) * rows, rows), rows)
        item_keep[k * rows : (k + 1) * rows, :] = item_acc[at, :]
        at = pl.ds(pl.multiple_of((me ^ other) * rows, rows), rows)
        encode(item_acc[at, :], item_send, k * (rows + EXTRA))


def chip_sum_kernel(keep, recv, total, level, cross):
    rows = total.shape[0]
    total[...] = keep[:rows, :] + recv[:rows, :]
    for k, (send, start) in enumerate(((level, 0), (cross, 0), (cross, rows + EXTRA)), 1):
        at = slice(k * rows, (k + 1) * rows)
        encode(keep[at, :] + recv[at, :], send, start)


def forward_kernel(recv, send):
    send[...] = recv[send.shape[0] :, :]


def relay_kernel(keep, recv, send):
    rows = keep.shape[0] // 2
    encode(keep[rows:, :] + decode(recv, rows + EXTRA, rows), send, 0)


def count_kernel(nbrs, _, adj, digits):
    counts_of(nbrs, adj, digits)


def smooth_kernel(n_user, n_item, user_adj, item_nbrs, *refs):
    user_in, refs = refs[:n_user], refs[n_user:]
    item_in, refs = refs[:n_item], refs[n_item:]
    user_own, item_own, _, user_out, item_out, users, items, *refs = refs
    item_adj, digits = refs
    place(user_in, item_in, users, items)
    counts_of(item_nbrs, item_adj, digits)
    for adj, whole, own, out in (
        (user_adj, users, user_own, user_out),
        (item_adj, items, item_own, item_out),
    ):
        near = lax.dot_general(
            whole[...], adj[...], (((0,), (0,)), ((), ())), preferred_element_type=jnp.float32
        )
        mine = own[: out.shape[0], :].astype(jnp.float32)
        out[...] = SMOOTH * (mine - near.T * (1.0 / 16))


def final_kernel(n_user, user_smooth, item_smooth, user_total, item_total, *refs):
    user_out, item_out = refs[-2:]
    parts = refs[:-2]
    for smooth, total, recv, out in (
        (user_smooth, user_total, parts[:n_user], user_out),
        (item_smooth, item_total, parts[n_user:], item_out),
    ):
        rows = out.shape[0]
        whole = total[:rows, :]
        for part in recv:
            whole = whole + decode(part, 0, rows)
        out[...] = DATA_SCALE * whole + smooth[...]


def swap(array, axis, size, even, odd=None):
    odd = even if odd is None else odd
    return lax.ppermute(array, axis, [(i, i ^ (odd if i % 2 else even)) for i in range(size)])


def local(
    n_row, n_col,
    user_factors, item_factors, ratings, tile_cell, keep_count, send_count, user_nbrs, item_nbrs
):
    f32, bf16, i16 = jnp.float32, jnp.bfloat16, jnp.int16
    user_own, item_own = user_factors, item_factors[0]
    user_rows, rank = user_own.shape
    item_rows = item_own.shape[0]
    block_users, block_items = user_rows * n_col, item_rows * n_row
    pin = lambda array: pltpu.with_memory_space_constraint(array, pltpu.HBM)
    knn = user_nbrs.shape[1]
    slots, tile = ratings.shape[2:4]
    direct = n_col == 8 and n_row == 4

    if direct:
        far = swap(item_own, "row", n_row, 2)
        other = swap(user_own, "col", n_col, 1)
        mark = call(
            mark_kernel, struct(8, 128, f32), [pin(ratings[0, 0])], "mark", spaces=[HBM],
            flops=COST_MARK,
        )
        user_pair, user_held = call(
            user_pair_kernel,
            [struct(2 * user_rows, rank, bf16), struct(user_rows, rank, bf16)],
            [user_own, other, mark],
            "user_pair",
            spaces=[VMEM, VMEM, ANY],
        )
        cross = tie(swap(user_pair, "col", n_col, 2, 6), COST_CROSS)
        level = tie(swap(user_held, "col", n_col, 4), COST_LEVEL)
        plan = call(
            plan_kernel,
            pltpu.SMEM((1 + slots,), jnp.int32),
            [keep_count, send_count, tile_cell, user_pair],
            "plan",
            spaces=[SMEM] * 3 + [ANY],
            results=SMEM,
            flops=COST_PLAN,
        )
        item_pair = call(
            pair_kernel,
            struct(2 * item_rows, rank, bf16),
            [item_own, far],
            "item_pair",
        )
        near = swap(item_pair, "row", n_row, 1)
        near = tie(near, COST_NEAR)
        user_in = [
            user_pair, level, swap(level, "col", n_col, 1), cross, swap(cross, "col", n_col, 1),
        ]
        item_in = [item_pair, near]
    else:
        item_in = [lax.all_gather(item_own, "row", axis=0, tiled=True)]
        user_in = [lax.all_gather(user_own, "col", axis=0, tiled=True)]
        plan = call(
            plan_kernel,
            pltpu.SMEM((1 + slots,), jnp.int32),
            [keep_count, send_count, tile_cell, item_in[0]],
            "plan",
            spaces=[SMEM] * 3 + [ANY],
            results=SMEM,
            flops=COST_PLAN,
        )

    if direct:
        outs = [
            struct(block_users // 2, rank, f32),
            struct(block_users // 2, rank, f32),
            struct(block_items // 2, rank, f32),
            struct(2 * (item_rows + EXTRA), rank, i16),
        ]
    else:
        outs = [struct(block_users, rank, f32), struct(block_items, rank, f32)]
    n_user, n_item = len(user_in), len(item_in)
    grads = call(
        functools.partial(main_kernel, n_user, n_item, direct),
        outs,
        [plan, ratings[0, 0]] + user_in + item_in,
        "tiles",
        spaces=[SMEM] + [VMEM] * (1 + n_user + n_item),
        scratch=[
            pltpu.VMEM((block_users, rank), bf16),
            pltpu.VMEM((block_items, rank), bf16),
            pltpu.VMEM((block_users, rank), f32),
            pltpu.VMEM((block_items, rank), f32),
        ],
        flops=6 * slots * tile * tile * rank,
        nbytes=ratings.size * 2,
        limit=24,
    )

    if direct:
        user_keep, user_send, item_keep, item_send = grads
        user_recv = swap(user_send, "col", n_col, 1)
        item_recv = swap(item_send, "row", n_row, 1)
        item_last = call(
            relay_kernel,
            struct(item_rows + EXTRA, rank, i16),
            [item_keep, item_recv],
            "item_relay",
            flops=COST_IF,
        )
        item_last = swap(item_last, "row", n_row, 2)
        user_total, level, cross = call(
            chip_sum_kernel,
            [
                struct(user_rows, rank, f32),
                struct(user_rows + EXTRA, rank, i16),
                struct(2 * (user_rows + EXTRA), rank, i16),
            ],
            [user_keep, user_recv],
            "chip_sum",
        )
        cross = swap(cross, "col", n_col, 2, 6)
        level = tie(swap(level, "col", n_col, 4), COST_RL)
        behind = call(
            forward_kernel, struct(user_rows + EXTRA, rank, i16), [cross], "forward",
            flops=COST_FW,
        )
        user_parts = [level, cross, swap(behind, "col", n_col, 1)]
        item_parts = [item_recv, item_last]
        item_total, early = item_keep, user_total
    else:
        user_total = lax.psum_scatter(grads[0], "col", scatter_dimension=0, tiled=True)
        item_total = lax.psum_scatter(grads[1], "row", scatter_dimension=0, tiled=True)
        user_parts, item_parts = [], []
        behind = early = user_total

    user_adj = call(
        count_kernel,
        struct(block_users, user_rows, bf16),
        [user_nbrs.T, early],
        "user_counts",
        spaces=[VMEM, ANY],
        scratch=[pltpu.VMEM((words_of(knn, block_users), knn, user_rows), jnp.int32)],
        flops=COST_UC,
    )
    own = [user_in[0], item_in[0]] if direct else [user_own, item_own]
    smooth = call(
        functools.partial(smooth_kernel, n_user, n_item),
        [struct(user_rows, rank, f32), struct(item_rows, rank, f32)],
        [user_adj, item_nbrs[0].T] + user_in + item_in + own + [behind],
        "smooth",
        spaces=[VMEM] * (4 + n_user + n_item) + [ANY],
        scratch=[
            pltpu.VMEM((block_users, rank), bf16),
            pltpu.VMEM((block_items, rank), bf16),
            pltpu.VMEM((block_items, item_rows), bf16),
            pltpu.VMEM((words_of(knn, block_items), knn, item_rows), jnp.int32),
        ],
        flops=COST_SMOOTH,
    )

    if direct:
        item_parts[1] = tie(item_parts[1], COST_IL, after=smooth[0])
    grad_users, grad_items = call(
        functools.partial(final_kernel, len(user_parts)),
        [struct(user_rows, rank, f32), struct(item_rows, rank, f32)],
        list(smooth) + [user_total, item_total] + user_parts + item_parts,
        "finish",
        flops=8 * (user_rows + item_rows) * rank,
        nbytes=20 * (user_rows + item_rows) * rank,
    )
    return (grad_users, grad_items[None])


def solution(mesh):
    placed = (
        P(("row", "col"), None),
        P("col", "row", None),
        P("row", "col", None, None, None),
        P("row", "col", None),
        P("row", "col"),
        P("row", "col", None),
        P(("row", "col"), None),
        P("col", "row", None),
    )
    return jax.shard_map(
        functools.partial(local, mesh.shape["row"], mesh.shape["col"]),
        mesh=mesh,
        in_specs=placed,
        out_specs=(P(("row", "col"), None), P("col", "row", None)),
        check_vma=False,
    )
```

```python
import functools

import jax
import jax.numpy as jnp
from jax import lax
from jax.experimental import pallas as pl
from jax.experimental.pallas import tpu as pltpu
from jax.sharding import PartitionSpec as P

ALPHA = 0.5
DATA_SCALE = 0.0625
SMOOTH = 4.0
GROUP = 36
COST_NEAR = 10**10
COST_LEVEL = 6*10**8
COST_CROSS = 0
COST_PLAN = 0
COST_SMOOTH = 0
COST_IF = 0
COST_MARK = 10**8
COST_UC = 0
COST_RL = 6*10**8
COST_FW = 0
COST_IL = 10**10
VMEM = pl.BlockSpec(memory_space=pltpu.VMEM)
ANY = pl.BlockSpec(memory_space=pl.ANY)
HBM = pl.BlockSpec(memory_space=pltpu.HBM)
SMEM = pl.BlockSpec(memory_space=pltpu.SMEM)


def call(kernel, outs, ins, name, spaces=None, results=None, scratch=(), flops=0, nbytes=0, limit=16):
    return pl.pallas_call(
        kernel,
        out_shape=outs,
        in_specs=spaces or [VMEM] * len(ins),
        out_specs=results or jax.tree.map(lambda _: VMEM, outs),
        scratch_shapes=scratch,
        cost_estimate=pl.CostEstimate(flops=flops, bytes_accessed=nbytes, transcendentals=0),
        compiler_params=pltpu.CompilerParams(vmem_limit_bytes=limit * 2**20),
        name=name,
    )(*ins)


def struct(rows, cols, dtype):
    return jax.ShapeDtypeStruct((rows, cols), dtype)


EXTRA = 16
OCTAVE = 64.0
TOP = 32400.0


def encode(block, out_ref, start):
    rows = block.shape[0]
    top = jnp.max(jnp.abs(block), axis=0, keepdims=True)
    level = jnp.ceil(jnp.log2(jnp.maximum(top, 1e-30)) * OCTAVE)
    fixed = jnp.round(block * (jnp.exp2(level * (-1.0 / OCTAVE)) * TOP))
    out_ref[start : start + rows, :] = fixed.astype(jnp.int32).astype(jnp.int16)
    spread = jnp.broadcast_to(level, (EXTRA, block.shape[1]))
    out_ref[start + rows : start + rows + EXTRA, :] = spread.astype(jnp.int32).astype(jnp.int16)


def decode(ref, start, rows):
    stop = start + rows
    level = ref[stop : stop + EXTRA, :].astype(jnp.int32).astype(jnp.float32)[:1]
    scale = jnp.exp2(level * (1.0 / OCTAVE)) * (1.0 / TOP)
    return ref[start:stop, :].astype(jnp.int32).astype(jnp.float32) * scale


def counts_of(nbrs, adj, digits):
    count, width = nbrs.shape
    blocks = adj.shape[0] // 128
    bits = count.bit_length()
    fields = 31 // bits
    words = -(-blocks // fields)
    step = 32
    index = nbrs[...]
    block = index >> 7
    digits[0] = index & 127
    for word in range(words):
        field = block - word * fields
        inside = (field >= 0) & (field < fields)
        digits[1 + word] = jnp.where(inside, 1 << (jnp.where(inside, field, 0) * bits), 0)
    for left in range(0, width, 128):
        lanes = slice(left, min(left + 128, width))
        span = lanes.stop - lanes.start

        def body(turn, _, lanes=lanes, span=span):
            here = turn * step + lax.broadcasted_iota(jnp.int32, (step, span), 0)
            totals = [jnp.zeros((step, span), jnp.int32)] * words
            for k in range(count):
                hit = jnp.broadcast_to(digits[0, k : k + 1, lanes], (step, span)) == here
                for word in range(words):
                    one = jnp.broadcast_to(digits[1 + word, k : k + 1, lanes], (step, span))
                    totals[word] = totals[word] + jnp.where(hit, one, 0)
            for block in range(blocks):
                word, field = divmod(block, fields)
                value = (totals[word] >> (field * bits)) & ((1 << bits) - 1)
                at = pl.ds(pl.multiple_of(block * 128 + turn * step, step), step)
                adj[at, lanes] = value.astype(jnp.float32).astype(jnp.bfloat16)
            return 0

        lax.fori_loop(0, 128 // step, body, 0)


def words_of(count, rows):
    return 1 + -(-(rows // 128) // (31 // count.bit_length()))


def plan_kernel(keep, sends, cells, _, plan):
    live = keep[0, 0]
    for q in range(sends.shape[2]):
        live = live + sends[0, 0, q]
    plan[0] = live
    for slot in range(cells.shape[2]):
        plan[1 + slot] = cells[0, 0, slot]


def mark_kernel(source, out):
    out[...] = jnp.zeros_like(out)


def user_pair_kernel(own, other, _, out, held):
    pair_kernel(own, other, out)
    held[...] = own[...]


def pair_kernel(own, other, out):
    rows = own.shape[0]
    out[:rows, :] = own[...]
    out[rows:, :] = other[...]


def tie_kernel(source, *refs):
    refs[-1][...] = source[...]


def tie(array, cost, after=None):
    if not cost:
        return array
    later = [] if after is None else [after]
    return call(
        tie_kernel,
        struct(*array.shape, array.dtype),
        [array] + later,
        "tie",
        spaces=[VMEM] + [ANY] * len(later),
        flops=cost,
    )


def col_masks():
    me = lax.axis_index("col")
    cross = 2 + 4 * (me & 1)
    return me, cross, 8 - cross


def place(user_in, item_in, users, items):
    if len(user_in) == 1:
        users[...] = user_in[0][...]
        items[...] = item_in[0][...]
        return
    pair, level, swap_level, cross, swap_cross = user_in
    me, mine, yours = col_masks()
    rows = level.shape[0]
    for ref, masks in (
        (pair, (0, 1)),
        (level, (4,)),
        (swap_level, (5,)),
        (cross, (mine, mine ^ 1)),
        (swap_cross, (yours ^ 1, yours)),
    ):
        for k, mask in enumerate(masks):
            at = pl.ds(pl.multiple_of((me ^ mask) * rows, rows), rows)
            users[at, :] = ref[k * rows : (k + 1) * rows, :]
    me = lax.axis_index("row")
    rows = item_in[0].shape[0] // 2
    for ref, masks in zip(item_in, ((0, 2), (1, 3))):
        for k, mask in enumerate(masks):
            at = pl.ds(pl.multiple_of((me ^ mask) * rows, rows), rows)
            items[at, :] = ref[k * rows : (k + 1) * rows, :]


def main_kernel(n_user, n_item, direct, plan, ratings, *refs):
    user_in, refs = refs[:n_user], refs[n_user:]
    item_in, refs = refs[:n_item], refs[n_item:]
    outs, (users, items, user_acc, item_acc) = refs[:-4], refs[-4:]
    slots, tile = ratings.shape[:2]
    group = max(g for g in range(1, GROUP + 1) if slots % g == 0)
    item_count = items.shape[0] // tile
    place(user_in, item_in, users, items)
    user_acc[...] = jnp.zeros_like(user_acc)
    item_acc[...] = jnp.zeros_like(item_acc)
    live = plan[0]

    def body(turn, _):
        work = []
        for g in range(group):
            slot = turn * group + g
            cell = plan[1 + slot]
            upper = cell // item_count
            lower = cell - upper * item_count
            user_at = pl.ds(pl.multiple_of(upper * tile, tile), tile)
            item_at = pl.ds(pl.multiple_of(lower * tile, tile), tile)
            left = users[user_at, :]
            right = items[item_at, :]
            product = lax.dot_general(
                left, right, (((1,), (1,)), ((), ())), preferred_element_type=jnp.float32
            )
            value = ratings[slot].astype(jnp.float32)
            error = (1.0 + ALPHA * value) * (product - jnp.where(value > 0, 1.0, 0.0))
            error = jnp.where(slot < live, error, 0.0).astype(jnp.bfloat16)
            work.append((user_at, item_at, left, right, error))
        for user_at, item_at, left, right, error in work:
            user_acc[user_at, :] += jnp.dot(error, right, preferred_element_type=jnp.float32)
            item_acc[item_at, :] += lax.dot_general(
                error, left, (((0,), (0,)), ((), ())), preferred_element_type=jnp.float32
            )
        return 0

    if group == slots:
        body(0, 0)
    else:
        lax.fori_loop(0, (live + group - 1) // group, body, 0)

    if not direct:
        outs[0][...] = user_acc[...]
        outs[1][...] = item_acc[...]
        return
    user_keep, user_send, item_keep, item_send = outs
    me, mine, yours = col_masks()
    rows = user_keep.shape[0] // 4
    for out, masks in (
        (user_keep, (0, 4, mine, mine ^ 1)),
        (user_send, (1, 5, yours ^ 1, yours)),
    ):
        for k, mask in enumerate(masks):
            at = pl.ds(pl.multiple_of((me ^ mask) * rows, rows), rows)
            out[k * rows : (k + 1) * rows, :] = user_acc[at, :]
    me = lax.axis_index("row")
    rows = item_keep.shape[0] // 2
    for k, (own, other) in enumerate(((0, 1), (2, 3))):
        at = pl.ds(pl.multiple_of((me ^ own) * rows, rows), rows)
        item_keep[k * rows : (k + 1) * rows, :] = item_acc[at, :]
        at = pl.ds(pl.multiple_of((me ^ other) * rows, rows), rows)
        encode(item_acc[at, :], item_send, k * (rows + EXTRA))


def chip_sum_kernel(keep, recv, total, level, cross):
    rows = total.shape[0]
    total[...] = keep[:rows, :] + recv[:rows, :]
    for k, (send, start) in enumerate(((level, 0), (cross, 0), (cross, rows + EXTRA)), 1):
        at = slice(k * rows, (k + 1) * rows)
        encode(keep[at, :] + recv[at, :], send, start)


def forward_kernel(recv, send):
    send[...] = recv[send.shape[0] :, :]


def relay_kernel(keep, recv, send):
    rows = keep.shape[0] // 2
    encode(keep[rows:, :] + decode(recv, rows + EXTRA, rows), send, 0)


def count_kernel(nbrs, _, adj, digits):
    counts_of(nbrs, adj, digits)


def smooth_kernel(n_user, n_item, user_adj, item_nbrs, *refs):
    user_in, refs = refs[:n_user], refs[n_user:]
    item_in, refs = refs[:n_item], refs[n_item:]
    user_own, item_own, _, user_out, item_out, users, items, *refs = refs
    item_adj, digits = refs
    place(user_in, item_in, users, items)
    counts_of(item_nbrs, item_adj, digits)
    for adj, whole, own, out in (
        (user_adj, users, user_own, user_out),
        (item_adj, items, item_own, item_out),
    ):
        near = lax.dot_general(
            whole[...], adj[...], (((0,), (0,)), ((), ())), preferred_element_type=jnp.float32
        )
        mine = own[: out.shape[0], :].astype(jnp.float32)
        out[...] = SMOOTH * (mine - near.T * (1.0 / 16))


def final_kernel(n_user, user_smooth, item_smooth, user_total, item_total, *refs):
    user_out, item_out = refs[-2:]
    parts = refs[:-2]
    for smooth, total, recv, out in (
        (user_smooth, user_total, parts[:n_user], user_out),
        (item_smooth, item_total, parts[n_user:], item_out),
    ):
        rows = out.shape[0]
        whole = total[:rows, :]
        for part in recv:
            whole = whole + decode(part, 0, rows)
        out[...] = DATA_SCALE * whole + smooth[...]


def swap(array, axis, size, even, odd=None):
    odd = even if odd is None else odd
    return lax.ppermute(array, axis, [(i, i ^ (odd if i % 2 else even)) for i in range(size)])


def local(
    n_row, n_col,
    user_factors, item_factors, ratings, tile_cell, keep_count, send_count, user_nbrs, item_nbrs
):
    f32, bf16, i16 = jnp.float32, jnp.bfloat16, jnp.int16
    user_own, item_own = user_factors, item_factors[0]
    user_rows, rank = user_own.shape
    item_rows = item_own.shape[0]
    block_users, block_items = user_rows * n_col, item_rows * n_row
    pin = lambda array: pltpu.with_memory_space_constraint(array, pltpu.HBM)
    knn = user_nbrs.shape[1]
    slots, tile = ratings.shape[2:4]
    direct = n_col == 8 and n_row == 4

    if direct:
        far = swap(item_own, "row", n_row, 2)
        other = swap(user_own, "col", n_col, 1)
        mark = call(
            mark_kernel, struct(8, 128, f32), [pin(ratings[0, 0])], "mark", spaces=[HBM],
            flops=COST_MARK,
        )
        user_pair, user_held = call(
            user_pair_kernel,
            [struct(2 * user_rows, rank, bf16), struct(user_rows, rank, bf16)],
            [user_own, other, mark],
            "user_pair",
            spaces=[VMEM, VMEM, ANY],
        )
        cross = tie(swap(user_pair, "col", n_col, 2, 6), COST_CROSS)
        level = tie(swap(user_held, "col", n_col, 4), COST_LEVEL)
        plan = call(
            plan_kernel,
            pltpu.SMEM((1 + slots,), jnp.int32),
            [keep_count, send_count, tile_cell, user_pair],
            "plan",
            spaces=[SMEM] * 3 + [ANY],
            results=SMEM,
            flops=COST_PLAN,
        )
        item_pair = call(
            pair_kernel,
            struct(2 * item_rows, rank, bf16),
            [item_own, far],
            "item_pair",
        )
        near = swap(item_pair, "row", n_row, 1)
        near = tie(near, COST_NEAR)
        user_in = [
            user_pair, level, swap(level, "col", n_col, 1), cross, swap(cross, "col", n_col, 1),
        ]
        item_in = [item_pair, near]
    else:
        item_in = [lax.all_gather(item_own, "row", axis=0, tiled=True)]
        user_in = [lax.all_gather(user_own, "col", axis=0, tiled=True)]
        plan = call(
            plan_kernel,
            pltpu.SMEM((1 + slots,), jnp.int32),
            [keep_count, send_count, tile_cell, item_in[0]],
            "plan",
            spaces=[SMEM] * 3 + [ANY],
            results=SMEM,
            flops=COST_PLAN,
        )

    if direct:
        outs = [
            struct(block_users // 2, rank, f32),
            struct(block_users // 2, rank, f32),
            struct(block_items // 2, rank, f32),
            struct(2 * (item_rows + EXTRA), rank, i16),
        ]
    else:
        outs = [struct(block_users, rank, f32), struct(block_items, rank, f32)]
    n_user, n_item = len(user_in), len(item_in)
    grads = call(
        functools.partial(main_kernel, n_user, n_item, direct),
        outs,
        [plan, ratings[0, 0]] + user_in + item_in,
        "tiles",
        spaces=[SMEM] + [VMEM] * (1 + n_user + n_item),
        scratch=[
            pltpu.VMEM((block_users, rank), bf16),
            pltpu.VMEM((block_items, rank), bf16),
            pltpu.VMEM((block_users, rank), f32),
            pltpu.VMEM((block_items, rank), f32),
        ],
        flops=6 * slots * tile * tile * rank,
        nbytes=ratings.size * 2,
        limit=24,
    )

    if direct:
        user_keep, user_send, item_keep, item_send = grads
        user_recv = swap(user_send, "col", n_col, 1)
        item_recv = swap(item_send, "row", n_row, 1)
        item_last = call(
            relay_kernel,
            struct(item_rows + EXTRA, rank, i16),
            [item_keep, item_recv],
            "item_relay",
            flops=COST_IF,
        )
        item_last = swap(item_last, "row", n_row, 2)
        user_total, level, cross = call(
            chip_sum_kernel,
            [
                struct(user_rows, rank, f32),
                struct(user_rows + EXTRA, rank, i16),
                struct(2 * (user_rows + EXTRA), rank, i16),
            ],
            [user_keep, user_recv],
            "chip_sum",
        )
        cross = swap(cross, "col", n_col, 2, 6)
        level = tie(swap(level, "col", n_col, 4), COST_RL)
        behind = call(
            forward_kernel, struct(user_rows + EXTRA, rank, i16), [cross], "forward",
            flops=COST_FW,
        )
        user_parts = [level, cross, swap(behind, "col", n_col, 1)]
        item_parts = [item_recv, item_last]
        item_total, early = item_keep, user_total
    else:
        user_total = lax.psum_scatter(grads[0], "col", scatter_dimension=0, tiled=True)
        item_total = lax.psum_scatter(grads[1], "row", scatter_dimension=0, tiled=True)
        user_parts, item_parts = [], []
        behind = early = user_total

    user_adj = call(
        count_kernel,
        struct(block_users, user_rows, bf16),
        [user_nbrs.T, early],
        "user_counts",
        spaces=[VMEM, ANY],
        scratch=[pltpu.VMEM((words_of(knn, block_users), knn, user_rows), jnp.int32)],
        flops=COST_UC,
    )
    own = [user_in[0], item_in[0]] if direct else [user_own, item_own]
    smooth = call(
        functools.partial(smooth_kernel, n_user, n_item),
        [struct(user_rows, rank, f32), struct(item_rows, rank, f32)],
        [user_adj, item_nbrs[0].T] + user_in + item_in + own + [behind],
        "smooth",
        spaces=[VMEM] * (4 + n_user + n_item) + [ANY],
        scratch=[
            pltpu.VMEM((block_users, rank), bf16),
            pltpu.VMEM((block_items, rank), bf16),
            pltpu.VMEM((block_items, item_rows), bf16),
            pltpu.VMEM((words_of(knn, block_items), knn, item_rows), jnp.int32),
        ],
        flops=COST_SMOOTH,
    )

    if direct:
        item_parts[1] = tie(item_parts[1], COST_IL, after=smooth[0])
    grad_users, grad_items = call(
        functools.partial(final_kernel, len(user_parts)),
        [struct(user_rows, rank, f32), struct(item_rows, rank, f32)],
        list(smooth) + [user_total, item_total] + user_parts + item_parts,
        "finish",
        flops=8 * (user_rows + item_rows) * rank,
        nbytes=20 * (user_rows + item_rows) * rank,
    )
    return (grad_users, grad_items[None])


def solution(mesh):
    placed = (
        P(("row", "col"), None),
        P("col", "row", None),
        P("row", "col", None, None, None),
        P("row", "col", None),
        P("row", "col"),
        P("row", "col", None),
        P(("row", "col"), None),
        P("col", "row", None),
    )
    return jax.shard_map(
        functools.partial(local, mesh.shape["row"], mesh.shape["col"]),
        mesh=mesh,
        in_specs=placed,
        out_specs=(P(("row", "col"), None), P("col", "row", None)),
        check_vma=False,
    )
```

```python
import functools

import jax
import jax.numpy as jnp
from jax import lax
from jax.experimental import pallas as pl
from jax.experimental.pallas import tpu as pltpu
from jax.sharding import PartitionSpec as P

ALPHA = 0.5
DATA_SCALE = 0.0625
SMOOTH = 4.0
GROUP = 36
COST_NEAR = 10**10
COST_LEVEL = 6*10**8
COST_CROSS = 0
COST_PLAN = 0
COST_SMOOTH = 0
COST_IF = 0
COST_MARK = 10**8
COST_UC = 0
COST_RL = 6*10**8
COST_FW = 0
COST_IL = 10**10
VMEM = pl.BlockSpec(memory_space=pltpu.VMEM)
ANY = pl.BlockSpec(memory_space=pl.ANY)
HBM = pl.BlockSpec(memory_space=pltpu.HBM)
SMEM = pl.BlockSpec(memory_space=pltpu.SMEM)


def call(kernel, outs, ins, name, spaces=None, results=None, scratch=(), flops=0, nbytes=0, limit=16):
    return pl.pallas_call(
        kernel,
        out_shape=outs,
        in_specs=spaces or [VMEM] * len(ins),
        out_specs=results or jax.tree.map(lambda _: VMEM, outs),
        scratch_shapes=scratch,
        cost_estimate=pl.CostEstimate(flops=flops, bytes_accessed=nbytes, transcendentals=0),
        compiler_params=pltpu.CompilerParams(vmem_limit_bytes=limit * 2**20),
        name=name,
    )(*ins)


def struct(rows, cols, dtype):
    return jax.ShapeDtypeStruct((rows, cols), dtype)


EXTRA = 16
OCTAVE = 64.0
TOP = 32400.0


def encode(block, out_ref, start):
    rows = block.shape[0]
    top = jnp.max(jnp.abs(block), axis=0, keepdims=True)
    level = jnp.ceil(jnp.log2(jnp.maximum(top, 1e-30)) * OCTAVE)
    fixed = jnp.round(block * (jnp.exp2(level * (-1.0 / OCTAVE)) * TOP))
    out_ref[start : start + rows, :] = fixed.astype(jnp.int32).astype(jnp.int16)
    spread = jnp.broadcast_to(level, (EXTRA, block.shape[1]))
    out_ref[start + rows : start + rows + EXTRA, :] = spread.astype(jnp.int32).astype(jnp.int16)


def decode(ref, start, rows):
    stop = start + rows
    level = ref[stop : stop + EXTRA, :].astype(jnp.int32).astype(jnp.float32)[:1]
    scale = jnp.exp2(level * (1.0 / OCTAVE)) * (1.0 / TOP)
    return ref[start:stop, :].astype(jnp.int32).astype(jnp.float32) * scale


def counts_of(nbrs, adj, digits):
    count, width = nbrs.shape
    blocks = adj.shape[0] // 128
    bits = count.bit_length()
    fields = 31 // bits
    words = -(-blocks // fields)
    step = 32
    index = nbrs[...]
    block = index >> 7
    digits[0] = index & 127
    for word in range(words):
        field = block - word * fields
        inside = (field >= 0) & (field < fields)
        digits[1 + word] = jnp.where(inside, 1 << (jnp.where(inside, field, 0) * bits), 0)
    for left in range(0, width, 128):
        lanes = slice(left, min(left + 128, width))
        span = lanes.stop - lanes.start

        def body(turn, _, lanes=lanes, span=span):
            here = turn * step + lax.broadcasted_iota(jnp.int32, (step, span), 0)
            totals = [jnp.zeros((step, span), jnp.int32)] * words
            for k in range(count):
                hit = jnp.broadcast_to(digits[0, k : k + 1, lanes], (step, span)) == here
                for word in range(words):
                    one = jnp.broadcast_to(digits[1 + word, k : k + 1, lanes], (step, span))
                    totals[word] = totals[word] + jnp.where(hit, one, 0)
            for block in range(blocks):
                word, field = divmod(block, fields)
                value = (totals[word] >> (field * bits)) & ((1 << bits) - 1)
                at = pl.ds(pl.multiple_of(block * 128 + turn * step, step), step)
                adj[at, lanes] = value.astype(jnp.float32).astype(jnp.bfloat16)
            return 0

        lax.fori_loop(0, 128 // step, body, 0)


def words_of(count, rows):
    return 1 + -(-(rows // 128) // (31 // count.bit_length()))


def plan_kernel(keep, sends, cells, _, plan):
    live = keep[0, 0]
    for q in range(sends.shape[2]):
        live = live + sends[0, 0, q]
    plan[0] = live
    for slot in range(cells.shape[2]):
        plan[1 + slot] = cells[0, 0, slot]


def mark_kernel(source, out):
    out[...] = jnp.zeros_like(out)


def user_pair_kernel(own, other, _, out, held):
    pair_kernel(own, other, out)
    held[...] = own[...]


def pair_kernel(own, other, out):
    rows = own.shape[0]
    out[:rows, :] = own[...]
    out[rows:, :] = other[...]


def tie_kernel(source, *refs):
    refs[-1][...] = source[...]


def tie(array, cost, after=None):
    if not cost:
        return array
    later = [] if after is None else [after]
    return call(
        tie_kernel,
        struct(*array.shape, array.dtype),
        [array] + later,
        "tie",
        spaces=[VMEM] + [ANY] * len(later),
        flops=cost,
    )


def col_masks():
    me = lax.axis_index("col")
    cross = 4 + 2 * (me & 1)
    return me, cross, 10 - cross


def place(user_in, item_in, users, items):
    if len(user_in) == 1:
        users[...] = user_in[0][...]
        items[...] = item_in[0][...]
        return
    pair, level, swap_level, cross, swap_cross = user_in
    me, mine, yours = col_masks()
    rows = level.shape[0]
    for ref, masks in (
        (pair, (0, 1)),
        (level, (2,)),
        (swap_level, (3,)),
        (cross, (mine, mine ^ 1)),
        (swap_cross, (yours ^ 1, yours)),
    ):
        for k, mask in enumerate(masks):
            at = pl.ds(pl.multiple_of((me ^ mask) * rows, rows), rows)
            users[at, :] = ref[k * rows : (k + 1) * rows, :]
    me = lax.axis_index("row")
    rows = item_in[0].shape[0] // 2
    for ref, masks in zip(item_in, ((0, 2), (1, 3))):
        for k, mask in enumerate(masks):
            at = pl.ds(pl.multiple_of((me ^ mask) * rows, rows), rows)
            items[at, :] = ref[k * rows : (k + 1) * rows, :]


def main_kernel(n_user, n_item, direct, plan, ratings, *refs):
    user_in, refs = refs[:n_user], refs[n_user:]
    item_in, refs = refs[:n_item], refs[n_item:]
    outs, (users, items, user_acc, item_acc) = refs[:-4], refs[-4:]
    slots, tile = ratings.shape[:2]
    group = max(g for g in range(1, GROUP + 1) if slots % g == 0)
    item_count = items.shape[0] // tile
    place(user_in, item_in, users, items)
    user_acc[...] = jnp.zeros_like(user_acc)
    item_acc[...] = jnp.zeros_like(item_acc)
    live = plan[0]

    def body(turn, _):
        work = []
        for g in range(group):
            slot = turn * group + g
            cell = plan[1 + slot]
            upper = cell // item_count
            lower = cell - upper * item_count
            user_at = pl.ds(pl.multiple_of(upper * tile, tile), tile)
            item_at = pl.ds(pl.multiple_of(lower * tile, tile), tile)
            left = users[user_at, :]
            right = items[item_at, :]
            product = lax.dot_general(
                left, right, (((1,), (1,)), ((), ())), preferred_element_type=jnp.float32
            )
            value = ratings[slot].astype(jnp.float32)
            error = (1.0 + ALPHA * value) * (product - jnp.where(value > 0, 1.0, 0.0))
            error = jnp.where(slot < live, error, 0.0).astype(jnp.bfloat16)
            work.append((user_at, item_at, left, right, error))
        for user_at, item_at, left, right, error in work:
            user_acc[user_at, :] += jnp.dot(error, right, preferred_element_type=jnp.float32)
            item_acc[item_at, :] += lax.dot_general(
                error, left, (((0,), (0,)), ((), ())), preferred_element_type=jnp.float32
            )
        return 0

    if group == slots:
        body(0, 0)
    else:
        lax.fori_loop(0, (live + group - 1) // group, body, 0)

    if not direct:
        outs[0][...] = user_acc[...]
        outs[1][...] = item_acc[...]
        return
    user_keep, user_send, item_keep, item_send = outs
    me, mine, yours = col_masks()
    rows = user_keep.shape[0] // 4
    for out, masks in (
        (user_keep, (0, 2, mine, mine ^ 1)),
        (user_send, (1, 3, yours ^ 1, yours)),
    ):
        for k, mask in enumerate(masks):
            at = pl.ds(pl.multiple_of((me ^ mask) * rows, rows), rows)
            out[k * rows : (k + 1) * rows, :] = user_acc[at, :]
    me = lax.axis_index("row")
    rows = item_keep.shape[0] // 2
    for k, (own, other) in enumerate(((0, 1), (2, 3))):
        at = pl.ds(pl.multiple_of((me ^ own) * rows, rows), rows)
        item_keep[k * rows : (k + 1) * rows, :] = item_acc[at, :]
        at = pl.ds(pl.multiple_of((me ^ other) * rows, rows), rows)
        encode(item_acc[at, :], item_send, k * (rows + EXTRA))


def chip_sum_kernel(keep, recv, total, level, cross):
    rows = total.shape[0]
    total[...] = keep[:rows, :] + recv[:rows, :]
    for k, (send, start) in enumerate(((level, 0), (cross, 0), (cross, rows + EXTRA)), 1):
        at = slice(k * rows, (k + 1) * rows)
        encode(keep[at, :] + recv[at, :], send, start)


def forward_kernel(recv, send):
    send[...] = recv[send.shape[0] :, :]


def relay_kernel(keep, recv, send):
    rows = keep.shape[0] // 2
    encode(keep[rows:, :] + decode(recv, rows + EXTRA, rows), send, 0)


def count_kernel(nbrs, _, adj, digits):
    counts_of(nbrs, adj, digits)


def smooth_kernel(n_user, n_item, user_adj, item_nbrs, *refs):
    user_in, refs = refs[:n_user], refs[n_user:]
    item_in, refs = refs[:n_item], refs[n_item:]
    user_own, item_own, _, user_out, item_out, users, items, *refs = refs
    item_adj, digits = refs
    place(user_in, item_in, users, items)
    counts_of(item_nbrs, item_adj, digits)
    for adj, whole, own, out in (
        (user_adj, users, user_own, user_out),
        (item_adj, items, item_own, item_out),
    ):
        near = lax.dot_general(
            whole[...], adj[...], (((0,), (0,)), ((), ())), preferred_element_type=jnp.float32
        )
        mine = own[: out.shape[0], :].astype(jnp.float32)
        out[...] = SMOOTH * (mine - near.T * (1.0 / 16))


def final_kernel(n_user, user_smooth, item_smooth, user_total, item_total, *refs):
    user_out, item_out = refs[-2:]
    parts = refs[:-2]
    for smooth, total, recv, out in (
        (user_smooth, user_total, parts[:n_user], user_out),
        (item_smooth, item_total, parts[n_user:], item_out),
    ):
        rows = out.shape[0]
        whole = total[:rows, :]
        for part in recv:
            whole = whole + decode(part, 0, rows)
        out[...] = DATA_SCALE * whole + smooth[...]


def swap(array, axis, size, even, odd=None):
    odd = even if odd is None else odd
    return lax.ppermute(array, axis, [(i, i ^ (odd if i % 2 else even)) for i in range(size)])


def local(
    n_row, n_col,
    user_factors, item_factors, ratings, tile_cell, keep_count, send_count, user_nbrs, item_nbrs
):
    f32, bf16, i16 = jnp.float32, jnp.bfloat16, jnp.int16
    user_own, item_own = user_factors, item_factors[0]
    user_rows, rank = user_own.shape
    item_rows = item_own.shape[0]
    block_users, block_items = user_rows * n_col, item_rows * n_row
    pin = lambda array: pltpu.with_memory_space_constraint(array, pltpu.HBM)
    knn = user_nbrs.shape[1]
    slots, tile = ratings.shape[2:4]
    direct = n_col == 8 and n_row == 4

    if direct:
        far = swap(item_own, "row", n_row, 2)
        other = swap(user_own, "col", n_col, 1)
        mark = call(
            mark_kernel, struct(8, 128, f32), [pin(ratings[0, 0])], "mark", spaces=[HBM],
            flops=COST_MARK,
        )
        user_pair, user_held = call(
            user_pair_kernel,
            [struct(2 * user_rows, rank, bf16), struct(user_rows, rank, bf16)],
            [user_own, other, mark],
            "user_pair",
            spaces=[VMEM, VMEM, ANY],
        )
        cross = tie(swap(user_pair, "col", n_col, 4, 6), COST_CROSS)
        level = tie(swap(user_held, "col", n_col, 2), COST_LEVEL)
        plan = call(
            plan_kernel,
            pltpu.SMEM((1 + slots,), jnp.int32),
            [keep_count, send_count, tile_cell, user_pair],
            "plan",
            spaces=[SMEM] * 3 + [ANY],
            results=SMEM,
            flops=COST_PLAN,
        )
        item_pair = call(
            pair_kernel,
            struct(2 * item_rows, rank, bf16),
            [item_own, far],
            "item_pair",
        )
        near = swap(item_pair, "row", n_row, 1)
        near = tie(near, COST_NEAR)
        user_in = [
            user_pair, level, swap(level, "col", n_col, 1), cross, swap(cross, "col", n_col, 1),
        ]
        item_in = [item_pair, near]
    else:
        item_in = [lax.all_gather(item_own, "row", axis=0, tiled=True)]
        user_in = [lax.all_gather(user_own, "col", axis=0, tiled=True)]
        plan = call(
            plan_kernel,
            pltpu.SMEM((1 + slots,), jnp.int32),
            [keep_count, send_count, tile_cell, item_in[0]],
            "plan",
            spaces=[SMEM] * 3 + [ANY],
            results=SMEM,
            flops=COST_PLAN,
        )

    if direct:
        outs = [
            struct(block_users // 2, rank, f32),
            struct(block_users // 2, rank, f32),
            struct(block_items // 2, rank, f32),
            struct(2 * (item_rows + EXTRA), rank, i16),
        ]
    else:
        outs = [struct(block_users, rank, f32), struct(block_items, rank, f32)]
    n_user, n_item = len(user_in), len(item_in)
    grads = call(
        functools.partial(main_kernel, n_user, n_item, direct),
        outs,
        [plan, ratings[0, 0]] + user_in + item_in,
        "tiles",
        spaces=[SMEM] + [VMEM] * (1 + n_user + n_item),
        scratch=[
            pltpu.VMEM((block_users, rank), bf16),
            pltpu.VMEM((block_items, rank), bf16),
            pltpu.VMEM((block_users, rank), f32),
            pltpu.VMEM((block_items, rank), f32),
        ],
        flops=6 * slots * tile * tile * rank,
        nbytes=ratings.size * 2,
        limit=24,
    )

    if direct:
        user_keep, user_send, item_keep, item_send = grads
        user_recv = swap(user_send, "col", n_col, 1)
        item_recv = swap(item_send, "row", n_row, 1)
        item_last = call(
            relay_kernel,
            struct(item_rows + EXTRA, rank, i16),
            [item_keep, item_recv],
            "item_relay",
            flops=COST_IF,
        )
        item_last = swap(item_last, "row", n_row, 2)
        user_total, level, cross = call(
            chip_sum_kernel,
            [
                struct(user_rows, rank, f32),
                struct(user_rows + EXTRA, rank, i16),
                struct(2 * (user_rows + EXTRA), rank, i16),
            ],
            [user_keep, user_recv],
            "chip_sum",
        )
        cross = swap(cross, "col", n_col, 4, 6)
        level = tie(swap(level, "col", n_col, 2), COST_RL)
        behind = call(
            forward_kernel, struct(user_rows + EXTRA, rank, i16), [cross], "forward",
            flops=COST_FW,
        )
        user_parts = [level, cross, swap(behind, "col", n_col, 1)]
        item_parts = [item_recv, item_last]
        item_total, early = item_keep, user_total
    else:
        user_total = lax.psum_scatter(grads[0], "col", scatter_dimension=0, tiled=True)
        item_total = lax.psum_scatter(grads[1], "row", scatter_dimension=0, tiled=True)
        user_parts, item_parts = [], []
        behind = early = user_total

    user_adj = call(
        count_kernel,
        struct(block_users, user_rows, bf16),
        [user_nbrs.T, early],
        "user_counts",
        spaces=[VMEM, ANY],
        scratch=[pltpu.VMEM((words_of(knn, block_users), knn, user_rows), jnp.int32)],
        flops=COST_UC,
    )
    own = [user_in[0], item_in[0]] if direct else [user_own, item_own]
    smooth = call(
        functools.partial(smooth_kernel, n_user, n_item),
        [struct(user_rows, rank, f32), struct(item_rows, rank, f32)],
        [user_adj, item_nbrs[0].T] + user_in + item_in + own + [behind],
        "smooth",
        spaces=[VMEM] * (4 + n_user + n_item) + [ANY],
        scratch=[
            pltpu.VMEM((block_users, rank), bf16),
            pltpu.VMEM((block_items, rank), bf16),
            pltpu.VMEM((block_items, item_rows), bf16),
            pltpu.VMEM((words_of(knn, block_items), knn, item_rows), jnp.int32),
        ],
        flops=COST_SMOOTH,
    )

    if direct:
        item_parts[1] = tie(item_parts[1], COST_IL, after=smooth[0])
    grad_users, grad_items = call(
        functools.partial(final_kernel, len(user_parts)),
        [struct(user_rows, rank, f32), struct(item_rows, rank, f32)],
        list(smooth) + [user_total, item_total] + user_parts + item_parts,
        "finish",
        flops=8 * (user_rows + item_rows) * rank,
        nbytes=20 * (user_rows + item_rows) * rank,
    )
    return (grad_users, grad_items[None])


def solution(mesh):
    placed = (
        P(("row", "col"), None),
        P("col", "row", None),
        P("row", "col", None, None, None),
        P("row", "col", None),
        P("row", "col"),
        P("row", "col", None),
        P(("row", "col"), None),
        P("col", "row", None),
    )
    return jax.shard_map(
        functools.partial(local, mesh.shape["row"], mesh.shape["col"]),
        mesh=mesh,
        in_specs=placed,
        out_specs=(P(("row", "col"), None), P("col", "row", None)),
        check_vma=False,
    )
```
